32 devices in a mesh: rack: 4 (over x, core), node: 8 (over z, y).
Axes of the slice: x: 2, y: 2, z: 4, core: 2. Of those that a mesh axis runs over, the one named last changes fastest.
Arguments:
- stored: bfloat16 [640, 8, 4096], P(('rack', 'node')), may hold values from -6 to 6
- coefficients: bfloat16 [64, 10, 8, 8], replicated, may hold values from -0.3 to 0.61
- helper_rack: int32 [64, 10], replicated, may hold values from 0 to 3, as said below
- helper_node: int32 [64, 10], replicated, may hold values from 0 to 7, as said below
- helper_block: int32 [64, 10], replicated, may hold values from 0 to 19, as said below
Outputs:
- rebuilt: float32 [64, 8, 4096], P(('rack', 'node'))
The draws below stay inside these ranges and needn't reach their ends.
Inputs may be any that keep to these rules, and one draw needn't show every extreme that they name: Repair r is rebuilt on device r // 2, counted rack-major. Its 10 helpers are distinct devices other than that one. With devices counted rack-major as helper_rack * 8 + helper_node, (helper device minus owner device) mod (32) depends only on h and r mod 2. `helper_node`: follows the same rule as helper_rack. `helper_block`: each of a device's 20 stored blocks is read by exactly one pair of repair and helper.
All inputs are finite; a program needn't handle non-finite values.
Results may differ from the reference program's by a relative error of at most 0.0003.
Values sent between devices are 32-bit elements; how exact they have to be, the bound alone decides.
A program may use at most 64 MiB of HBM per device.

```python
import math
import jax
import jax.numpy as jnp
from jax import lax

PLANES = 8
HELPERS = 10
REP_DEV = 2
REPAIRS = 64
HOLD = 20
LEN = 4096
N_RACK = 4
N_NODE = 8


def permute_slots(perm_key):
    return jax.random.permutation(perm_key, HOLD)


def routing(key):
    devices = N_RACK * N_NODE
    offset_keys = jax.random.split(jax.random.fold_in(key, 7001), REP_DEV)
    offsets = jnp.stack([jax.random.permutation(offset_keys[slot], devices - 1)[:HELPERS] + 1 for slot in range(REP_DEV)]).astype(jnp.int32)
    repair_ids = jnp.arange(REPAIRS, dtype=jnp.int32)
    owner = repair_ids // REP_DEV
    position = repair_ids % REP_DEV
    device = (owner[:, None] + offsets[position]) % devices
    rack = device // N_NODE
    node = device % N_NODE
    perm_keys = jax.random.split(jax.random.fold_in(key, 7002), devices)
    slot_perms = jax.vmap(permute_slots)(perm_keys).astype(jnp.int32)
    columns = jnp.arange(HELPERS, dtype=jnp.int32)[None, :] * REP_DEV + position[:, None]
    block = slot_perms[device, columns]
    return (rack.astype(jnp.int32), node.astype(jnp.int32), block.astype(jnp.int32))


def draw_helper_rack(key, part):
    return routing(key)[0]


def draw_helper_node(key, part):
    return routing(key)[1]


def draw_helper_block(key, part):
    return routing(key)[2]


def draw_coefficients(key, part):
    noise_key = jax.random.fold_in(key, 7003)
    shape = (REPAIRS, HELPERS, PLANES, PLANES)
    noise = jnp.clip(jax.random.normal(noise_key, shape, jnp.float32), -3.0, 3.0) * 0.3
    identity = jnp.eye(PLANES, dtype=jnp.float32)
    return ((identity + noise) / math.sqrt(HELPERS)).astype(jnp.bfloat16)


def block_levels(rng, shape, pieces, low, largest):
    factor_of, own = 1.0, jax.random.fold_in(rng, 6)
    for axis_at, shards_of in pieces:
        draws = jnp.exp(jax.random.uniform(jax.random.fold_in(own, axis_at), (shards_of,), jnp.float32, low / len(pieces), largest / len(pieces)))
        factor_of = factor_of * jnp.repeat(draws, shape[axis_at] // shards_of).reshape([-1 if axis == axis_at else 1 for axis in range(len(shape))])
    return factor_of


def scatter_about(rng, extent, width, most, pieces=(), kind=jnp.bfloat16):
    result = width * jax.random.normal(rng, extent, jnp.float32)
    if pieces:
        result = result * block_levels(rng, extent, pieces, -0.22, 0.18)
    return jnp.clip(result, -most, most).astype(kind)


def setup_inputs(seed: int = 0) -> dict:
    key_of = jax.random.split(jax.random.key(seed), 6)
    return {
        "stored": scatter_about(key_of[0], (N_RACK * N_NODE * HOLD, PLANES, LEN), 1.0, 6.0, ((0, 32),)),
        "coefficients": draw_coefficients(jax.random.fold_in(key_of[5], 71), 0),
        "helper_rack": draw_helper_rack(jax.random.fold_in(key_of[5], 71), 0),
        "helper_node": draw_helper_node(jax.random.fold_in(key_of[5], 71), 0),
        "helper_block": draw_helper_block(jax.random.fold_in(key_of[5], 71), 0),
    }


def reference(stored, coefficients, helper_rack, helper_node, helper_block):
    source_rows = ((helper_rack * N_NODE + helper_node) * HOLD + helper_block).astype(jnp.int32)

    def repair(packed):
        row_index, coeffs = packed
        partial_value = jnp.zeros((PLANES, LEN), jnp.float32)
        for helper_pos in range(HELPERS):
            source = stored[row_index[helper_pos]].astype(jnp.float32)
            partial_value = partial_value + jnp.dot(coeffs[helper_pos].astype(jnp.float32), source, precision=lax.Precision.HIGHEST)
        return partial_value

    return lax.map(repair, (source_rows, coefficients))
```

```python
import functools

import jax
import jax.numpy as jnp
from jax import lax
from jax.experimental import pallas as pl
from jax.experimental.pallas import tpu as pltpu
from jax.sharding import PartitionSpec as P

MESH = pl.DeviceIdType.MESH
CORES = 2
CHUNKS = 4


def repair_kernel(
    sizes,
    marks_ref,
    coeffs_ref,
    stored_ref,
    out_ref,
    weights,
    wide,
    fetched,
    first,
    mid_x,
    mid_y,
    last_x,
    last_y,
    ending,
    core_send,
    core_recv,
    one_send,
    one_recv,
    two_send,
    two_recv,
    three_send,
    three_recv,
):
    nx, ny, nz, helpers, hold, planes, own_rows, width = sizes
    rack, node = lax.axis_index("rack"), lax.axis_index("node")
    x, core = lax.div(rack, CORES), lax.rem(rack, CORES)
    z, y = lax.div(node, ny), lax.rem(node, ny)

    def at_core(step):
        return (x * CORES + lax.rem(core + step, CORES), node)

    def to_x(step):
        return lax.rem(x + step, nx)

    def to_y(step):
        return lax.rem(y + step, ny)

    def to_z(step):
        return lax.rem(z + step, nz)

    def at_x(step):
        return (to_x(step) * CORES + core, node)

    def at_y(step):
        return (rack, z * ny + to_y(step))

    def at_z(step):
        return (rack, to_z(step) * ny + y)

    peers = (
        [at_core(1)]
        + [at_x(s) for s in range(1, nx)]
        + [at_y(s) for s in range(1, ny)]
        + [at_z(s) for s in range(1, nz)]
    )
    barrier = pltpu.get_barrier_semaphore()
    for peer in peers:
        pl.semaphore_signal(barrier, inc=1, device_id=peer, device_id_type=MESH)
    pl.semaphore_wait(barrier, len(peers))

    def remote(source, target, send, recv, device):
        return pltpu.make_async_remote_copy(
            src_ref=source,
            dst_ref=target,
            send_sem=send,
            recv_sem=recv,
            device_id=device,
            device_id_type=MESH,
        )

    def lanes(half, chunk):
        return pl.ds((half * CHUNKS + chunk) * width, width)

    def core_copy(half, chunk):
        return remote(
            wide.at[half, chunk],
            fetched.at[half, chunk],
            core_send.at[half, chunk],
            core_recv.at[half, chunk],
            at_core(1),
        )

    for chunk in range(CHUNKS):
        for half in range(2):
            wide[half, chunk] = stored_ref[:, lanes(half, chunk)].astype(jnp.float32)
            core_copy(half, chunk).start()

    blocks = hold * planes
    group = own_rows // nx
    repairs = group // planes
    column = lax.broadcasted_iota(jnp.int32, (group, blocks), 1)
    column_block = lax.div(column, planes)
    spread_row = lax.broadcasted_iota(jnp.int32, (planes, blocks), 0)
    spread_column = lax.broadcasted_iota(jnp.int32, (planes, blocks), 1)
    spread = (lax.rem(spread_column, planes) == spread_row).astype(jnp.bfloat16)
    for gx in range(nx):
        rack_of = gx * CORES + core
        mine = jnp.zeros((group, blocks), jnp.float32)
        theirs = jnp.zeros((group, blocks), jnp.float32)
        marks = marks_ref[pl.ds(rack_of * group, group), :]
        for helper in range(helpers):
            small = coeffs_ref[pl.ds(rack_of * repairs, repairs), helper]
            small = small.astype(jnp.float32).reshape(group, planes)
            tiled = jnp.dot(
                small.astype(jnp.bfloat16), spread, preferred_element_type=jnp.float32
            )
            mark = marks[:, helper : helper + 1]
            mine = jnp.where(mark == column_block, tiled, mine)
            theirs = jnp.where(mark - hold == column_block, tiled, theirs)
        weights[0, gx * group : (gx + 1) * group, :] = mine.astype(jnp.bfloat16)
        weights[1, gx * group : (gx + 1) * group, :] = theirs.astype(jnp.bfloat16)

    def copies_one(half, chunk):
        if half == 0:
            return [
                remote(
                    first.at[half, chunk, to_x(s)],
                    mid_x.at[chunk, s - 1],
                    one_send.at[half, chunk, s - 1],
                    one_recv.at[half, chunk, s - 1],
                    at_x(s),
                )
                for s in range(1, nx)
            ]
        return [
            remote(
                first.at[half, chunk, :, :, to_y(s)],
                mid_y.at[chunk, s - 1],
                one_send.at[half, chunk, s - 1],
                one_recv.at[half, chunk, s - 1],
                at_y(s),
            )
            for s in range(1, ny)
        ]

    def copies_two(half, chunk):
        if half == 0:
            return [
                remote(
                    mid_x.at[chunk, 0, :, to_y(s)],
                    last_x.at[chunk, s - 1],
                    two_send.at[half, chunk, s - 1],
                    two_recv.at[half, chunk, s - 1],
                    at_y(s),
                )
                for s in range(1, ny)
            ]
        return [
            remote(
                mid_y.at[chunk, 0, to_x(s)],
                last_y.at[chunk, s - 1],
                two_send.at[half, chunk, s - 1],
                two_recv.at[half, chunk, s - 1],
                at_x(s),
            )
            for s in range(1, nx)
        ]

    def copies_three(half, chunk):
        last = last_x if half == 0 else last_y
        return [
            remote(
                last.at[chunk, 0, to_z(s)],
                ending.at[half, chunk, s - 1],
                three_send.at[half, chunk, s - 1],
                three_recv.at[half, chunk, s - 1],
                at_z(s),
            )
            for s in range(1, nz)
        ]

    def stage_one(half, chunk):
        core_copy(half, chunk).wait_recv()
        near = stored_ref[:, lanes(half, chunk)]
        far = fetched[half, chunk].astype(jnp.bfloat16)
        total = jnp.dot(weights[0], near, preferred_element_type=jnp.float32)
        total += jnp.dot(weights[1], far, preferred_element_type=jnp.float32)
        first[half, chunk] = total.reshape(first.shape[2:])
        for copy in copies_one(half, chunk):
            copy.start()

    def stage_two(half, chunk):
        copies = copies_one(half, chunk)
        for copy in copies:
            copy.wait_recv()
        mid = mid_x if half == 0 else mid_y
        if half == 0:
            total = first[half, chunk, x]
        else:
            total = first[half, chunk, :, :, y]
        for slot in range(len(copies)):
            total += mid[chunk, slot]
        mid[chunk, 0] = total
        for copy in copies_two(half, chunk):
            copy.start()

    def stage_three(half, chunk):
        copies = copies_two(half, chunk)
        for copy in copies:
            copy.wait_recv()
        last = last_x if half == 0 else last_y
        if half == 0:
            total = mid_x[chunk, 0, :, y]
        else:
            total = mid_y[chunk, 0, x]
        for slot in range(len(copies)):
            total += last[chunk, slot]
        last[chunk, 0] = total
        for copy in copies_three(half, chunk):
            copy.start()

    def stage_four(half, chunk):
        copies = copies_three(half, chunk)
        for copy in copies:
            copy.wait_recv()
        last = last_x if half == 0 else last_y
        total = last[chunk, 0, z]
        for slot in range(len(copies)):
            total += ending[half, chunk, slot]
        out_ref[:, lanes(half, chunk)] = total

    stages = (stage_one, stage_two, stage_three, stage_four)
    for tick in range(CHUNKS + len(stages) - 1):
        for depth, stage in enumerate(stages):
            chunk = tick - depth
            if 0 <= chunk < CHUNKS:
                for half in range(2):
                    stage(half, chunk)

    for chunk in range(CHUNKS):
        for half in range(2):
            core_copy(half, chunk).wait_send()
            for copies in (copies_one, copies_two, copies_three):
                for copy in copies(half, chunk):
                    copy.wait_send()


def solution(mesh):
    racks, nodes = mesh.shape["rack"], mesh.shape["node"]
    nx, ny = racks // CORES, 2
    nz = nodes // ny

    def on_device(stored, coefficients, helper_rack, helper_node, helper_block):
        hold, planes, length = stored.shape
        repairs, helpers = helper_block.shape
        rep_dev = repairs // (racks * nodes)
        out_rows = rep_dev * planes
        own_rows = repairs * planes // CORES
        width = length // (2 * CHUNKS)
        rack, node = lax.axis_index("rack"), lax.axis_index("node")
        other = rack + 1 - 2 * lax.rem(rack, CORES)
        here = helper_node == node
        marks = jnp.where(
            here & (helper_rack == rack),
            helper_block,
            jnp.where(here & (helper_rack == other), helper_block + hold, -1),
        )
        marks = jnp.broadcast_to(marks[:, None, :], (repairs, planes, helpers))
        marks = marks.reshape(repairs * planes, helpers)
        sizes = (nx, ny, nz, helpers, hold, planes, own_rows, width)
        most = max(nx, ny) - 1
        dma = pltpu.SemaphoreType.DMA
        vmem = pl.BlockSpec(memory_space=pltpu.VMEM)
        rebuilt = pl.pallas_call(
            functools.partial(repair_kernel, sizes),
            out_shape=jax.ShapeDtypeStruct((out_rows, length), jnp.float32),
            in_specs=[vmem] * 3,
            out_specs=vmem,
            scratch_shapes=[
                pltpu.VMEM((2, own_rows, hold * planes), jnp.bfloat16),
                pltpu.VMEM((2, CHUNKS, hold * planes, width), jnp.float32),
                pltpu.VMEM((2, CHUNKS, hold * planes, width), jnp.float32),
                pltpu.VMEM((2, CHUNKS, nx, nz, ny, out_rows, width), jnp.float32),
                pltpu.VMEM((CHUNKS, nx - 1, nz, ny, out_rows, width), jnp.float32),
                pltpu.VMEM((CHUNKS, ny - 1, nx, nz, out_rows, width), jnp.float32),
                pltpu.VMEM((CHUNKS, ny - 1, nz, out_rows, width), jnp.float32),
                pltpu.VMEM((CHUNKS, nx - 1, nz, out_rows, width), jnp.float32),
                pltpu.VMEM((2, CHUNKS, nz - 1, out_rows, width), jnp.float32),
                dma((2, CHUNKS)),
                dma((2, CHUNKS)),
                dma((2, CHUNKS, most)),
                dma((2, CHUNKS, most)),
                dma((2, CHUNKS, most)),
                dma((2, CHUNKS, most)),
                dma((2, CHUNKS, nz - 1)),
                dma((2, CHUNKS, nz - 1)),
            ],
            compiler_params=pltpu.CompilerParams(
                collective_id=0,
                has_side_effects=True,
                vmem_limit_bytes=56 * 1024 * 1024,
            ),
        )(marks, coefficients, stored.reshape(hold * planes, length))
        return rebuilt.reshape(rep_dev, planes, length)

    return jax.shard_map(
        on_device,
        mesh=mesh,
        in_specs=(P(("rack", "node"), None, None), P(), P(), P(), P()),
        out_specs=P(("rack", "node"), None, None),
        check_vma=False,
    )
```

```python
import functools

import jax
import jax.numpy as jnp
from jax import lax
from jax.experimental import pallas as pl
from jax.experimental.pallas import tpu as pltpu
from jax.sharding import PartitionSpec as P

MESH = pl.DeviceIdType.MESH
CORES = 2
TILE = 128
AXES = ("x", "z", "y")


def lay_out(length):
    tiles = length // TILE
    side = tiles // 8
    widths = []
    left = (tiles - side) // 2
    while left:
        widths.append(min(2, left))
        left -= widths[-1]
    spare = tiles - 2 * sum(widths)
    groups, start = [], 0
    for number, wide in enumerate(widths):
        tasks, at = [], start
        plan = [("xyz", wide), ("yxz", wide)]
        if spare:
            plan.append((("zxy", "zyx")[number % 2], 1))
            spare -= 1
        for order, count in plan:
            tasks.append((order, at * TILE, count * TILE))
            at += count
        groups.append((start * TILE, (at - start) * TILE, tasks))
        start = at
    return groups


def repair_kernel(
    sizes,
    groups,
    rack_ref,
    node_ref,
    block_ref,
    coeffs_ref,
    stored_ref,
    out_ref,
    weights,
    core_send,
    core_recv,
    task_send,
    task_recv,
    *buffers,
):
    counts, helpers, hold, planes, repairs, per_rack = sizes
    ny = counts["y"]
    tasks = [task for group in groups for task in group[2]]
    wide, fetched = buffers[: len(groups)], buffers[len(groups) : 2 * len(groups)]
    held = buffers[2 * len(groups) :]
    held = [held[4 * t : 4 * t + 4] for t in range(len(tasks))]

    rack, node = lax.axis_index("rack"), lax.axis_index("node")
    core = lax.rem(rack, CORES)
    place = {"x": lax.div(rack, CORES), "z": lax.div(node, ny), "y": lax.rem(node, ny)}

    def moved(axis, step):
        return lax.rem(place[axis] + step, counts[axis])

    def device(axis, step):
        to = dict(place)
        to[axis] = moved(axis, step)
        return (to["x"] * CORES + core, to["z"] * ny + to["y"])

    other_rack = place["x"] * CORES + lax.rem(core + 1, CORES)
    other_core = (other_rack, node)
    peers = [other_core] + [device(a, s) for a in AXES for s in range(1, counts[a])]
    barrier = pltpu.get_barrier_semaphore()
    for peer in peers:
        pl.semaphore_signal(barrier, inc=1, device_id=peer, device_id_type=MESH)
    pl.semaphore_wait(barrier, len(peers))

    def remote(source, target, send, recv, to):
        return pltpu.make_async_remote_copy(
            src_ref=source,
            dst_ref=target,
            send_sem=send,
            recv_sem=recv,
            device_id=to,
            device_id_type=MESH,
        )

    def core_copy(g):
        return remote(wide[g], fetched[g], core_send.at[g], core_recv.at[g], other_core)

    for g, (start, width, _) in enumerate(groups):
        wide[g][...] = stored_ref[:, start : start + width].astype(jnp.float32)
        core_copy(g).start()

    here = node_ref[...] == node
    marks = jnp.where(
        here & (rack_ref[...] == rack),
        block_ref[...],
        jnp.where(here & (rack_ref[...] == other_rack), block_ref[...] + hold, -1),
    )
    own_rows = repairs * planes // CORES
    row = lax.broadcasted_iota(jnp.int32, (own_rows, repairs), 0)
    row_plane, row_repair = lax.rem(row, planes), lax.div(row, planes)
    row_repair = (
        lax.div(row_repair, per_rack) * CORES + core
    ) * per_rack + lax.rem(row_repair, per_rack)
    hits = row_repair == lax.broadcasted_iota(jnp.int32, (own_rows, repairs), 1)
    slot = lax.broadcasted_iota(jnp.int32, (2 * hold, planes, repairs), 0)
    summed = [jnp.zeros((own_rows, hold * planes), jnp.float32)] * 2
    for plane in range(planes):
        spread = jnp.zeros((2 * hold, planes, repairs), jnp.float32)
        for helper in range(helpers):
            values = coeffs_ref[helper, plane].astype(jnp.float32)[None]
            mark = marks[helper : helper + 1, :][None]
            spread = jnp.where(slot == mark, values, spread)
        spread = spread.reshape(2 * hold * planes, repairs).astype(jnp.bfloat16)
        picked = (hits & (row_plane == plane)).astype(jnp.float32).astype(jnp.bfloat16)
        for part in range(2):
            summed[part] += lax.dot_general(
                picked,
                spread[part * hold * planes : (part + 1) * hold * planes],
                (((1,), (1,)), ((), ())),
                preferred_element_type=jnp.float32,
            )
    for part in range(2):
        weights[part] = summed[part].astype(jnp.bfloat16)

    def before(t, stage):
        order = tasks[t][0]
        left = [axis for axis in AXES if axis not in order[:stage]]
        ahead = (slice(None),) * left.index(order[stage])
        if stage == 0:
            return held[t][0], lambda at: ahead + (at,)
        return held[t][stage], lambda at: (0,) + ahead + (at,)

    def copies(t, stage):
        axis = tasks[t][0][stage]
        source, pick = before(t, stage)
        return [
            remote(
                source.at[pick(moved(axis, s))],
                held[t][stage + 1].at[s - 1],
                task_send.at[t, stage, s - 1],
                task_recv.at[t, stage, s - 1],
                device(axis, s),
            )
            for s in range(1, counts[axis])
        ]

    def gathered(t, stage):
        axis = tasks[t][0][stage]
        source, pick = before(t, stage)
        arrived = copies(t, stage)
        for copy in arrived:
            copy.wait_recv()
        total = source[pick(place[axis])]
        for s in range(len(arrived)):
            total += held[t][stage + 1][s]
        return total

    def begin(g):
        start, width, inside = groups[g]
        core_copy(g).wait_recv()
        near = stored_ref[:, start : start + width]
        far = fetched[g][...].astype(jnp.bfloat16)
        total = jnp.dot(weights[0], near, preferred_element_type=jnp.float32)
        total += jnp.dot(weights[1], far, preferred_element_type=jnp.float32)
        for t in members[g]:
            _, at, count = tasks[t]
            piece = total[:, at - start : at - start + count]
            held[t][0][...] = piece.reshape(held[t][0].shape)
            for copy in copies(t, 0):
                copy.start()

    def advance(g, stage):
        for t in members[g]:
            held[t][stage][0] = gathered(t, stage - 1)
            for copy in copies(t, stage):
                copy.start()

    def finish(g):
        for t in members[g]:
            _, at, count = tasks[t]
            out_ref[:, at : at + count] = gathered(t, len(AXES) - 1)

    members, seen = [], 0
    for _, _, inside in groups:
        members.append(range(seen, seen + len(inside)))
        seen += len(inside)
    steps = (
        begin,
        functools.partial(advance, stage=1),
        functools.partial(advance, stage=2),
        finish,
    )
    for tick in range(len(groups) + len(steps) - 1):
        for depth, step in enumerate(steps):
            if 0 <= tick - depth < len(groups):
                step(tick - depth)

    for g in range(len(groups)):
        core_copy(g).wait_send()
        for t in members[g]:
            for stage in range(len(AXES)):
                for copy in copies(t, stage):
                    copy.wait_send()


def solution(mesh):
    racks, nodes = mesh.shape["rack"], mesh.shape["node"]
    counts = {"x": racks // CORES, "y": 2, "z": nodes // 2}

    def on_device(stored, coefficients, helper_rack, helper_node, helper_block):
        hold, planes, length = stored.shape
        repairs, helpers = helper_block.shape
        out_rows = repairs // (racks * nodes) * planes
        groups = lay_out(length)
        tasks = [task for group in groups for task in group[2]]
        sizes = (counts, helpers, hold, planes, repairs, repairs // racks)
        buffers = [
            pltpu.VMEM((hold * planes, width), jnp.float32)
            for _ in range(2)
            for _, width, _ in groups
        ]
        for order, _, width in tasks:
            for stage in range(len(AXES) + 1):
                left = [counts[a] for a in AXES if a not in order[:stage]]
                if stage:
                    left = [counts[order[stage - 1]] - 1] + left
                buffers.append(pltpu.VMEM((*left, out_rows, width), jnp.float32))
        most = max(counts.values()) - 1
        dma = pltpu.SemaphoreType.DMA
        vmem = pl.BlockSpec(memory_space=pltpu.VMEM)
        rebuilt = pl.pallas_call(
            functools.partial(repair_kernel, sizes, groups),
            out_shape=jax.ShapeDtypeStruct((out_rows, length), jnp.float32),
            in_specs=[vmem] * 5,
            out_specs=vmem,
            scratch_shapes=[
                pltpu.VMEM((2, repairs * planes // CORES, hold * planes), jnp.bfloat16),
                dma((len(groups),)),
                dma((len(groups),)),
                dma((len(tasks), len(AXES), most)),
                dma((len(tasks), len(AXES), most)),
                *buffers,
            ],
            compiler_params=pltpu.CompilerParams(
                collective_id=0,
                has_side_effects=True,
                vmem_limit_bytes=56 * 1024 * 1024,
            ),
        )(
            helper_rack.T,
            helper_node.T,
            helper_block.T,
            coefficients.transpose(1, 2, 3, 0),
            stored.reshape(hold * planes, length),
        )
        return rebuilt.reshape(-1, planes, length)

    return jax.shard_map(
        on_device,
        mesh=mesh,
        in_specs=(P(("rack", "node"), None, None), P(), P(), P(), P()),
        out_specs=P(("rack", "node"), None, None),
        check_vma=False,
    )
```

```python
import functools
import math

import jax
import jax.numpy as jnp
from jax import lax
from jax.experimental import pallas as pl
from jax.experimental.pallas import tpu as pltpu
from jax.sharding import PartitionSpec as P

MESH = pl.DeviceIdType.MESH
CORES = 2
TILE = 128
AXES = ("x", "z", "y")


def lay_out(length):
    tiles = length // TILE
    side = tiles // 8
    widths = []
    left = (tiles - side) // 2
    while left:
        widths.append(2 if left > 2 else 1)
        left -= widths[-1]
    spare = tiles - 2 * sum(widths)
    groups, start = [], 0
    for number, wide in enumerate(widths):
        tasks, at = [], start
        plan = [("xyz", wide), ("yxz", wide)]
        if spare:
            plan.append((("zxy", "zyx")[number % 2], 1))
            spare -= 1
        for order, count in plan:
            tasks.append((order, at * TILE, count * TILE))
            at += count
        groups.append((start * TILE, (at - start) * TILE, tasks))
        start = at
    return groups


def repair_kernel(
    sizes,
    groups,
    rack_ref,
    node_ref,
    block_ref,
    coeffs_ref,
    stored_ref,
    out_ref,
    weights,
    core_send,
    core_recv,
    task_send,
    task_recv,
    *buffers,
):
    counts, helpers, hold, planes, repairs, per_rack = sizes
    ny = counts["y"]
    tasks = [task for group in groups for task in group[2]]
    wide, fetched = buffers[: len(groups)], buffers[len(groups) : 2 * len(groups)]
    held = buffers[2 * len(groups) :]
    held = [held[4 * t : 4 * t + 4] for t in range(len(tasks))]

    rack, node = lax.axis_index("rack"), lax.axis_index("node")
    core = lax.rem(rack, CORES)
    place = {"x": lax.div(rack, CORES), "z": lax.div(node, ny), "y": lax.rem(node, ny)}

    def moved(axis, step):
        return lax.rem(place[axis] + step, counts[axis])

    def device(axis, step):
        to = dict(place)
        to[axis] = moved(axis, step)
        return (to["x"] * CORES + core, to["z"] * ny + to["y"])

    other_rack = place["x"] * CORES + lax.rem(core + 1, CORES)
    other_core = (other_rack, node)
    peers = [other_core] + [device(a, s) for a in AXES for s in range(1, counts[a])]
    barrier = pltpu.get_barrier_semaphore()
    for peer in peers:
        pl.semaphore_signal(barrier, inc=1, device_id=peer, device_id_type=MESH)

    def remote(source, target, send, recv, to):
        return pltpu.make_async_remote_copy(
            src_ref=source,
            dst_ref=target,
            send_sem=send,
            recv_sem=recv,
            device_id=to,
            device_id_type=MESH,
        )

    def core_copy(g):
        return remote(wide[g], fetched[g], core_send.at[g], core_recv.at[g], other_core)

    for g, (start, width, _) in enumerate(groups):
        wide[g][...] = stored_ref[:, start : start + width].astype(jnp.float32)

    here = node_ref[...] == node
    marks = jnp.where(
        here & (rack_ref[...] == rack),
        block_ref[...],
        jnp.where(here & (rack_ref[...] == other_rack), block_ref[...] + hold, -1),
    )
    own_rows = repairs * planes // CORES
    row = lax.broadcasted_iota(jnp.int32, (own_rows, repairs), 0)
    row_plane, row_repair = lax.rem(row, planes), lax.div(row, planes)
    row_repair = (
        lax.div(row_repair, per_rack) * CORES + core
    ) * per_rack + lax.rem(row_repair, per_rack)
    hits = row_repair == lax.broadcasted_iota(jnp.int32, (own_rows, repairs), 1)
    slot = lax.broadcasted_iota(jnp.int32, (2 * hold, planes, repairs), 0)
    summed = [jnp.zeros((own_rows, hold * planes), jnp.float32)] * 2
    for plane in range(planes):
        if plane == planes // 2:
            pl.semaphore_wait(barrier, len(peers))
            for g in range(len(groups)):
                core_copy(g).start()
        spread = jnp.zeros((2 * hold, planes, repairs), jnp.float32)
        for helper in range(helpers):
            values = coeffs_ref[helper, plane].astype(jnp.float32)[None]
            mark = marks[helper : helper + 1, :][None]
            spread = jnp.where(slot == mark, values, spread)
        spread = spread.reshape(2 * hold * planes, repairs).astype(jnp.bfloat16)
        picked = (hits & (row_plane == plane)).astype(jnp.float32).astype(jnp.bfloat16)
        for part in range(2):
            summed[part] += lax.dot_general(
                picked,
                spread[part * hold * planes : (part + 1) * hold * planes],
                (((1,), (1,)), ((), ())),
                preferred_element_type=jnp.float32,
            )
    for part in range(2):
        weights[part] = summed[part].astype(jnp.bfloat16)

    def before(t, stage):
        order = tasks[t][0]
        left = [axis for axis in AXES if axis not in order[:stage]]
        ahead = (slice(None),) * left.index(order[stage])
        if stage == 0:
            return held[t][0], lambda at: ahead + (at,)
        return held[t][stage], lambda at: (0,) + ahead + (at,)

    def copies(t, stage):
        axis = tasks[t][0][stage]
        source, pick = before(t, stage)
        return [
            remote(
                source.at[pick(moved(axis, s))],
                held[t][stage + 1].at[s - 1],
                task_send.at[t, stage, s - 1],
                task_recv.at[t, stage, s - 1],
                device(axis, s),
            )
            for s in range(1, counts[axis])
        ]

    def gathered(t, stage):
        axis = tasks[t][0][stage]
        source, pick = before(t, stage)
        arrived = copies(t, stage)
        for copy in arrived:
            copy.wait_recv()
        total = source[pick(place[axis])]
        for s in range(len(arrived)):
            total += held[t][stage + 1][s]
        return total

    def begin(g):
        start, width, inside = groups[g]
        core_copy(g).wait_recv()
        near = stored_ref[:, start : start + width]
        far = fetched[g][...].astype(jnp.bfloat16)
        total = jnp.dot(weights[0], near, preferred_element_type=jnp.float32)
        total += jnp.dot(weights[1], far, preferred_element_type=jnp.float32)
        for t in members[g]:
            _, at, count = tasks[t]
            piece = total[:, at - start : at - start + count]
            held[t][0][...] = piece.reshape(held[t][0].shape)
            for copy in copies(t, 0):
                copy.start()

    def advance(g, stage):
        for t in members[g]:
            held[t][stage][0] = gathered(t, stage - 1)
            for copy in copies(t, stage):
                copy.start()

    def finish(g):
        for t in members[g]:
            _, at, count = tasks[t]
            out_ref[:, at : at + count] = gathered(t, len(AXES) - 1)

    members, seen = [], 0
    for _, _, inside in groups:
        members.append(range(seen, seen + len(inside)))
        seen += len(inside)
    steps = (
        begin,
        functools.partial(advance, stage=1),
        functools.partial(advance, stage=2),
        finish,
    )
    delays = (0, 1, 2, 6)
    for tick in range(len(groups) + delays[-1]):
        for delay, step in zip(delays, steps):
            if 0 <= tick - delay < len(groups):
                step(tick - delay)

    for g in range(len(groups)):
        core_copy(g).wait_send()
        for t in members[g]:
            for stage in range(len(AXES)):
                for copy in copies(t, stage):
                    copy.wait_send()


def solution(mesh):
    racks, nodes = mesh.shape["rack"], mesh.shape["node"]
    counts = {"x": racks // CORES, "y": 2, "z": nodes // 2}

    def on_device(stored, coefficients, helper_rack, helper_node, helper_block):
        hold, planes, length = stored.shape
        repairs, helpers = helper_block.shape
        out_rows = repairs // (racks * nodes) * planes
        groups = lay_out(length)
        tasks = [task for group in groups for task in group[2]]
        sizes = (counts, helpers, hold, planes, repairs, repairs // racks)
        buffers = [
            pltpu.VMEM((hold * planes, width), jnp.float32)
            for _ in range(2)
            for _, width, _ in groups
        ]
        for order, _, width in tasks:
            for stage in range(len(AXES) + 1):
                left = [counts[a] for a in AXES if a not in order[:stage]]
                if stage:
                    left = [counts[order[stage - 1]] - 1] + left
                buffers.append(pltpu.VMEM((*left, out_rows, width), jnp.float32))
        most = max(counts.values()) - 1
        dma = pltpu.SemaphoreType.DMA
        vmem = pl.BlockSpec(memory_space=pltpu.VMEM)
        operands = (
            helper_rack.T,
            helper_node.T,
            helper_block.T,
            coefficients.transpose(1, 2, 3, 0),
            stored.reshape(hold * planes, length),
        )
        buffer_bytes = sum(math.prod(b.shape) * 4 for b in buffers)
        rebuilt = pl.pallas_call(
            functools.partial(repair_kernel, sizes, groups),
            out_shape=jax.ShapeDtypeStruct((out_rows, length), jnp.float32),
            in_specs=[vmem] * len(operands),
            out_specs=vmem,
            scratch_shapes=[
                pltpu.VMEM((2, repairs * planes // CORES, hold * planes), jnp.bfloat16),
                dma((len(groups),)),
                dma((len(groups),)),
                dma((len(tasks), len(AXES), most)),
                dma((len(tasks), len(AXES), most)),
                *buffers,
            ],
            compiler_params=pltpu.CompilerParams(
                collective_id=0,
                has_side_effects=True,
                vmem_limit_bytes=buffer_bytes + 12 * 1024 * 1024,
            ),
        )(*operands)
        return rebuilt.reshape(-1, planes, length)

    return jax.shard_map(
        on_device,
        mesh=mesh,
        in_specs=(P(("rack", "node"), None, None), P(), P(), P(), P()),
        out_specs=P(("rack", "node"), None, None),
        check_vma=False,
    )
```

```python
import functools
import math

import jax
import jax.numpy as jnp
from jax import lax
from jax.experimental import pallas as pl
from jax.experimental.pallas import tpu as pltpu
from jax.sharding import PartitionSpec as P

MESH = pl.DeviceIdType.MESH
CORES = 2
TILE = 128


def split_z(size):
    axes, stride = [], 1
    while size > 1:
        part = 2 if size % 2 == 0 else size
        axes.append((f"z{len(axes)}", part, stride))
        size, stride = size // part, stride * part
    return axes


def lay_out(length, along_z):
    plane = (("x", "y"), ("y", "x"))
    tiles = length // TILE
    side = tiles * 3 // 16
    widths = []
    left = (tiles - side) // 2
    while left:
        widths.append(2 if left > 2 else 1)
        left -= widths[-1]
    spare = tiles - 2 * sum(widths)
    groups, start = [], 0
    for number, wide in enumerate(widths):
        tasks, at = [], start
        plan = [(order + along_z, wide) for order in plane]
        if spare:
            plan.append((along_z + plane[number % 2], 1))
            spare -= 1
        for order, count in plan:
            tasks.append((order, at * TILE, count * TILE))
            at += count
        groups.append((start * TILE, (at - start) * TILE, tasks))
        start = at
    return groups


def repair_kernel(
    sizes,
    groups,
    rack_hbm,
    node_hbm,
    block_hbm,
    coeffs_hbm,
    stored_hbm,
    out_ref,
    rack_ref,
    node_ref,
    block_ref,
    coeffs_ref,
    stored_ref,
    copy_in,
    weights,
    core_send,
    core_recv,
    task_send,
    task_recv,
    *buffers,
):
    counts, z_axes, helpers, hold, planes, repairs, per_rack = sizes
    ny = counts["y"]
    axes = tuple(counts)
    tasks = [task for group in groups for task in group[2]]
    wide, fetched = buffers[: len(groups)], buffers[len(groups) : 2 * len(groups)]
    held = buffers[2 * len(groups) :]
    depth = len(axes) + 1
    held = [held[depth * t : depth * (t + 1)] for t in range(len(tasks))]

    rack, node = lax.axis_index("rack"), lax.axis_index("node")
    core = lax.rem(rack, CORES)
    place = {"x": lax.div(rack, CORES), "y": lax.rem(node, ny)}
    for name, size, stride in z_axes:
        place[name] = lax.rem(lax.div(node, ny * stride), size)

    def moved(axis, step):
        return lax.rem(place[axis] + step, counts[axis])

    def device(axis, step):
        to = dict(place)
        to[axis] = moved(axis, step)
        z = sum(to[name] * stride for name, _, stride in z_axes)
        return (to["x"] * CORES + core, z * ny + to["y"])

    other_rack = place["x"] * CORES + lax.rem(core + 1, CORES)
    other_core = (other_rack, node)
    peers = [other_core] + [device(a, s) for a in axes for s in range(1, counts[a])]
    barrier = pltpu.get_barrier_semaphore()
    for peer in peers:
        pl.semaphore_signal(barrier, inc=1, device_id=peer, device_id_type=MESH)

    arrays = (
        (stored_hbm, stored_ref),
        (rack_hbm, rack_ref),
        (node_hbm, node_ref),
        (block_hbm, block_ref),
        (coeffs_hbm, coeffs_ref),
    )
    loads = [
        pltpu.make_async_copy(source, target, copy_in.at[i])
        for i, (source, target) in enumerate(arrays)
    ]
    for load in loads:
        load.start()

    def remote(source, target, send, recv, to):
        return pltpu.make_async_remote_copy(
            src_ref=source,
            dst_ref=target,
            send_sem=send,
            recv_sem=recv,
            device_id=to,
            device_id_type=MESH,
        )

    def core_copy(g):
        return remote(wide[g], fetched[g], core_send.at[g], core_recv.at[g], other_core)

    loads[0].wait()
    for g, (start, width, _) in enumerate(groups):
        wide[g][...] = stored_ref[:, start : start + width].astype(jnp.float32)
    for load in loads[1:]:
        load.wait()

    here = node_ref[...] == node
    marks = jnp.where(
        here & (rack_ref[...] == rack),
        block_ref[...],
        jnp.where(here & (rack_ref[...] == other_rack), block_ref[...] + hold, -1),
    )
    own_rows = repairs * planes // CORES
    row = lax.broadcasted_iota(jnp.int32, (own_rows, repairs), 0)
    row_plane, row_repair = lax.rem(row, planes), lax.div(row, planes)
    row_repair = (
        lax.div(row_repair, per_rack) * CORES + core
    ) * per_rack + lax.rem(row_repair, per_rack)
    hits = row_repair == lax.broadcasted_iota(jnp.int32, (own_rows, repairs), 1)
    slot = lax.broadcasted_iota(jnp.int32, (2 * hold, planes, repairs), 0)
    summed = [jnp.zeros((own_rows, hold * planes), jnp.float32)] * 2
    for plane in range(planes):
        if plane == planes // 2:
            pl.semaphore_wait(barrier, len(peers))
            for g in range(len(groups)):
                core_copy(g).start()
        spread = jnp.zeros((2 * hold, planes, repairs), jnp.float32)
        for helper in range(helpers):
            values = coeffs_ref[helper, plane].astype(jnp.float32)[None]
            mark = marks[helper : helper + 1, :][None]
            spread = jnp.where(slot == mark, values, spread)
        spread = spread.reshape(2 * hold * planes, repairs).astype(jnp.bfloat16)
        picked = (hits & (row_plane == plane)).astype(jnp.float32).astype(jnp.bfloat16)
        for part in range(2):
            summed[part] += lax.dot_general(
                picked,
                spread[part * hold * planes : (part + 1) * hold * planes],
                (((1,), (1,)), ((), ())),
                preferred_element_type=jnp.float32,
            )
    for part in range(2):
        weights[part] = summed[part].astype(jnp.bfloat16)

    def before(t, stage):
        order = tasks[t][0]
        left = [axis for axis in axes if axis not in order[:stage]]
        ahead = (slice(None),) * left.index(order[stage])
        if stage == 0:
            return held[t][0], lambda at: ahead + (at,)
        return held[t][stage], lambda at: (0,) + ahead + (at,)

    def copies(t, stage):
        axis = tasks[t][0][stage]
        source, pick = before(t, stage)
        return [
            remote(
                source.at[pick(moved(axis, s))],
                held[t][stage + 1].at[s - 1],
                task_send.at[t, stage, s - 1],
                task_recv.at[t, stage, s - 1],
                device(axis, s),
            )
            for s in range(1, counts[axis])
        ]

    def gathered(t, stage):
        axis = tasks[t][0][stage]
        source, pick = before(t, stage)
        arrived = copies(t, stage)
        for copy in arrived:
            copy.wait_recv()
        total = source[pick(place[axis])]
        for s in range(len(arrived)):
            total += held[t][stage + 1][s]
        return total

    def begin(g):
        start, width, inside = groups[g]
        core_copy(g).wait_recv()
        near = stored_ref[:, start : start + width]
        far = fetched[g][...].astype(jnp.bfloat16)
        total = jnp.dot(weights[0], near, preferred_element_type=jnp.float32)
        total += jnp.dot(weights[1], far, preferred_element_type=jnp.float32)
        for t in members[g]:
            _, at, count = tasks[t]
            piece = total[:, at - start : at - start + count]
            held[t][0][...] = piece.reshape(held[t][0].shape)
            for copy in copies(t, 0):
                copy.start()

    def advance(g, stage):
        for t in members[g]:
            held[t][stage][0] = gathered(t, stage - 1)
            for copy in copies(t, stage):
                copy.start()

    def finish(g):
        for t in members[g]:
            _, at, count = tasks[t]
            out_ref[:, at : at + count] = gathered(t, len(axes) - 1)

    members, seen = [], 0
    for _, _, inside in groups:
        members.append(range(seen, seen + len(inside)))
        seen += len(inside)
    steps = (
        begin,
        *[functools.partial(advance, stage=stage) for stage in range(1, len(axes))],
        finish,
    )
    delays = (*range(len(axes)), len(axes) + 3)
    for tick in range(len(groups) + delays[-1]):
        for delay, step in zip(delays, steps):
            if 0 <= tick - delay < len(groups):
                step(tick - delay)

    for g in range(len(groups)):
        core_copy(g).wait_send()
        for t in members[g]:
            for stage in range(len(axes)):
                for copy in copies(t, stage):
                    copy.wait_send()


def solution(mesh):
    racks, nodes = mesh.shape["rack"], mesh.shape["node"]
    z_axes = split_z(nodes // 2)
    counts = {"x": racks // CORES}
    counts.update({name: size for name, size, _ in reversed(z_axes)})
    counts["y"] = 2

    def on_device(stored, coefficients, helper_rack, helper_node, helper_block):
        hold, planes, length = stored.shape
        repairs, helpers = helper_block.shape
        out_rows = repairs // (racks * nodes) * planes
        groups = lay_out(length, tuple(name for name, _, _ in z_axes))
        tasks = [task for group in groups for task in group[2]]
        sizes = (counts, z_axes, helpers, hold, planes, repairs, repairs // racks)
        buffers = [
            pltpu.VMEM((hold * planes, width), jnp.float32)
            for _ in range(2)
            for _, width, _ in groups
        ]
        for order, _, width in tasks:
            for stage in range(len(counts) + 1):
                left = [counts[a] for a in counts if a not in order[:stage]]
                if stage:
                    left = [counts[order[stage - 1]] - 1] + left
                buffers.append(pltpu.VMEM((*left, out_rows, width), jnp.float32))
        most = max(counts.values()) - 1
        dma = pltpu.SemaphoreType.DMA
        hbm = pl.BlockSpec(memory_space=pltpu.HBM)
        operands = (
            helper_rack.T,
            helper_node.T,
            helper_block.T,
            coefficients.transpose(1, 2, 3, 0),
            stored.reshape(hold * planes, length),
        )
        buffer_bytes = sum(math.prod(b.shape) * 4 for b in buffers)
        rebuilt = pl.pallas_call(
            functools.partial(repair_kernel, sizes, groups),
            out_shape=jax.ShapeDtypeStruct((out_rows, length), jnp.float32),
            in_specs=[hbm] * 5,
            out_specs=pl.BlockSpec(memory_space=pltpu.VMEM),
            scratch_shapes=[
                *[pltpu.VMEM(a.shape, a.dtype) for a in operands],
                dma((len(operands),)),
                pltpu.VMEM((2, repairs * planes // CORES, hold * planes), jnp.bfloat16),
                dma((len(groups),)),
                dma((len(groups),)),
                dma((len(tasks), len(counts), most)),
                dma((len(tasks), len(counts), most)),
                *buffers,
            ],
            compiler_params=pltpu.CompilerParams(
                collective_id=0,
                has_side_effects=True,
                vmem_limit_bytes=max(buffer_bytes + 12 * 2**20, 56 * 2**20),
            ),
        )(*operands)
        return rebuilt.reshape(-1, planes, length)

    return jax.shard_map(
        on_device,
        mesh=mesh,
        in_specs=(P(("rack", "node"), None, None), P(), P(), P(), P()),
        out_specs=P(("rack", "node"), None, None),
        check_vma=False,
    )
```

```python
import functools
import math

import jax
import jax.numpy as jnp
from jax import lax
from jax.experimental import pallas as pl
from jax.experimental.pallas import tpu as pltpu
from jax.sharding import PartitionSpec as P

MESH = pl.DeviceIdType.MESH
CORES = 2
TILE = 128


def split_z(size):
    axes, stride = [], 1
    while size > 1:
        part = 2 if size % 2 == 0 else size
        axes.append((f"z{len(axes)}", part, stride))
        size, stride = size // part, stride * part
    return axes


def lay_out(length, along_z):
    plane = (("x", "y"), ("y", "x"))
    tiles = length // TILE
    side = tiles * 3 // 16
    widths = [1]
    left = (tiles - side) // 2 - 1
    while left:
        widths.append(2 if left > 3 else 1)
        left -= widths[-1]
    spare = tiles - 2 * sum(widths)
    groups, start = [], 0
    for number, wide in enumerate(widths):
        tasks, at = [], start
        plan = [(order + along_z, wide) for order in plane]
        if spare:
            plan.append((along_z + plane[number % 2], 1))
            spare -= 1
        for order, count in plan:
            tasks.append((order, at * TILE, count * TILE))
            at += count
        groups.append((start * TILE, (at - start) * TILE, tasks))
        start = at
    return groups


def repair_kernel(
    sizes,
    groups,
    rack_hbm,
    node_hbm,
    block_hbm,
    coeffs_hbm,
    stored_hbm,
    own_ref,
    came_ref,
    rack_ref,
    node_ref,
    block_ref,
    coeffs_ref,
    stored_ref,
    copy_in,
    weights,
    core_send,
    core_recv,
    task_send,
    task_recv,
    *buffers,
):
    counts, z_axes, helpers, hold, planes, repairs, per_rack = sizes
    ny = counts["y"]
    axes = tuple(counts)
    tasks = [task for group in groups for task in group[2]]
    wide, fetched = buffers[: len(groups)], buffers[len(groups) : 2 * len(groups)]
    held = buffers[2 * len(groups) :]
    depth = len(axes) + 1
    held = [held[depth * t : depth * (t + 1)] for t in range(len(tasks))]

    rack, node = lax.axis_index("rack"), lax.axis_index("node")
    core = lax.rem(rack, CORES)
    place = {"x": lax.div(rack, CORES), "y": lax.rem(node, ny)}
    for name, size, stride in z_axes:
        place[name] = lax.rem(lax.div(node, ny * stride), size)

    def moved(axis, step):
        return lax.rem(place[axis] + step, counts[axis])

    def device(axis, step):
        to = dict(place)
        to[axis] = moved(axis, step)
        z = sum(to[name] * stride for name, _, stride in z_axes)
        return (to["x"] * CORES + core, z * ny + to["y"])

    other_rack = place["x"] * CORES + lax.rem(core + 1, CORES)
    other_core = (other_rack, node)
    peers = [other_core] + [device(a, s) for a in axes for s in range(1, counts[a])]
    barrier = pltpu.get_barrier_semaphore()
    for peer in peers:
        pl.semaphore_signal(barrier, inc=1, device_id=peer, device_id_type=MESH)

    arrays = (
        (rack_hbm, rack_ref),
        (node_hbm, node_ref),
        (block_hbm, block_ref),
        (coeffs_hbm, coeffs_ref),
        (stored_hbm, stored_ref),
    )
    loads = [
        pltpu.make_async_copy(source, target, copy_in.at[i])
        for i, (source, target) in enumerate(arrays)
    ]
    for load in loads:
        load.start()

    def remote(source, target, send, recv, to):
        return pltpu.make_async_remote_copy(
            src_ref=source,
            dst_ref=target,
            send_sem=send,
            recv_sem=recv,
            device_id=to,
            device_id_type=MESH,
        )

    def core_copy(g):
        return remote(wide[g], fetched[g], core_send.at[g], core_recv.at[g], other_core)

    for load in loads[:-1]:
        load.wait()

    here = node_ref[...] == node
    marks = jnp.where(
        here & (rack_ref[...] == rack),
        block_ref[...],
        jnp.where(here & (rack_ref[...] == other_rack), block_ref[...] + hold, -1),
    )
    own_rows = repairs * planes // CORES
    row = lax.broadcasted_iota(jnp.int32, (own_rows, 2 * repairs), 0)
    column = lax.broadcasted_iota(jnp.int32, (own_rows, 2 * repairs), 1)
    row_plane, row_repair = lax.rem(row, planes), lax.div(row, planes)
    row_repair = (
        lax.div(row_repair, per_rack) * CORES + core
    ) * per_rack + lax.rem(row_repair, per_rack)
    hits = row_repair == lax.rem(column, repairs)
    half = planes // 2
    hit_plane = row_plane - lax.div(column, repairs) * half
    marks = jnp.concatenate([marks, marks], axis=1)
    slot = lax.broadcasted_iota(jnp.int32, (2 * hold, planes, 2 * repairs), 0)
    summed = [jnp.zeros((own_rows, hold * planes), jnp.float32)] * 2
    for plane in range(half):
        if plane == half // 2:
            loads[-1].wait()
            for g, (start, width, _) in enumerate(groups):
                piece = stored_ref[:, start : start + width]
                wide[g][...] = piece.astype(jnp.float32)
            pl.semaphore_wait(barrier, len(peers))
            for g in range(len(groups)):
                core_copy(g).start()
        spread = jnp.zeros((2 * hold, planes, 2 * repairs), jnp.float32)
        for helper in range(helpers):
            values = [coeffs_ref[helper, plane + k * half] for k in range(2)]
            values = [value.astype(jnp.float32) for value in values]
            mark = marks[helper : helper + 1, :][None]
            spread = jnp.where(
                slot == mark, jnp.concatenate(values, axis=1)[None], spread
            )
        spread = spread.reshape(2 * hold * planes, 2 * repairs).astype(jnp.bfloat16)
        picked = (hits & (hit_plane == plane)).astype(jnp.float32).astype(jnp.bfloat16)
        for part in range(2):
            summed[part] += lax.dot_general(
                picked,
                spread[part * hold * planes : (part + 1) * hold * planes],
                (((1,), (1,)), ((), ())),
                preferred_element_type=jnp.float32,
            )
    for part in range(2):
        weights[part] = summed[part].astype(jnp.bfloat16)

    def before(t, stage):
        order = tasks[t][0]
        left = [axis for axis in axes if axis not in order[:stage]]
        ahead = (slice(None),) * left.index(order[stage])
        if stage == 0:
            return held[t][0], lambda at: ahead + (at,)
        return held[t][stage], lambda at: (0,) + ahead + (at,)

    def copies(t, stage):
        axis = tasks[t][0][stage]
        source, pick = before(t, stage)
        return [
            remote(
                source.at[pick(moved(axis, s))],
                held[t][stage + 1].at[s - 1],
                task_send.at[t, stage, s - 1],
                task_recv.at[t, stage, s - 1],
                device(axis, s),
            )
            for s in range(1, counts[axis])
        ]

    def gathered(t, stage):
        axis = tasks[t][0][stage]
        source, pick = before(t, stage)
        arrived = copies(t, stage)
        for copy in arrived:
            copy.wait_recv()
        came = held[t][stage + 1][0]
        for s in range(1, len(arrived)):
            came += held[t][stage + 1][s]
        return source[pick(place[axis])], came

    def begin(g):
        start, width, inside = groups[g]
        core_copy(g).wait_recv()
        near = stored_ref[:, start : start + width]
        far = fetched[g][...].astype(jnp.bfloat16)
        total = jnp.dot(weights[0], near, preferred_element_type=jnp.float32)
        total += jnp.dot(weights[1], far, preferred_element_type=jnp.float32)
        for t in members[g]:
            _, at, count = tasks[t]
            piece = total[:, at - start : at - start + count]
            held[t][0][...] = piece.reshape(held[t][0].shape)
            for copy in copies(t, 0):
                copy.start()

    def advance(g, stage):
        for t in members[g]:
            own, came = gathered(t, stage - 1)
            held[t][stage][0] = own + came
            for copy in copies(t, stage):
                copy.start()

    def finish(g):
        for t in members[g]:
            _, at, count = tasks[t]
            own, came = gathered(t, len(axes) - 1)
            own_ref[:, at : at + count] = own
            came_ref[:, at : at + count] = came

    members, seen = [], 0
    for _, _, inside in groups:
        members.append(range(seen, seen + len(inside)))
        seen += len(inside)
    steps = (
        begin,
        *[functools.partial(advance, stage=stage) for stage in range(1, len(axes))],
        finish,
    )
    delays = (*range(len(axes)), len(axes) + 3)
    for tick in range(len(groups) + delays[-1]):
        for delay, step in zip(delays, steps):
            if 0 <= tick - delay < len(groups):
                step(tick - delay)

    for g in range(len(groups)):
        core_copy(g).wait_send()
        for t in members[g]:
            for stage in range(len(axes)):
                for copy in copies(t, stage):
                    copy.wait_send()


def solution(mesh):
    racks, nodes = mesh.shape["rack"], mesh.shape["node"]
    z_axes = split_z(nodes // 2)
    counts = {"x": racks // CORES}
    counts.update({name: size for name, size, _ in reversed(z_axes)})
    counts["y"] = 2

    def on_device(stored, coefficients, helper_rack, helper_node, helper_block):
        hold, planes, length = stored.shape
        repairs, helpers = helper_block.shape
        out_rows = repairs // (racks * nodes) * planes
        groups = lay_out(length, tuple(name for name, _, _ in z_axes))
        tasks = [task for group in groups for task in group[2]]
        sizes = (counts, z_axes, helpers, hold, planes, repairs, repairs // racks)
        buffers = [
            pltpu.VMEM((hold * planes, width), jnp.float32)
            for _ in range(2)
            for _, width, _ in groups
        ]
        for order, _, width in tasks:
            for stage in range(len(counts) + 1):
                left = [counts[a] for a in counts if a not in order[:stage]]
                if stage:
                    left = [counts[order[stage - 1]] - 1] + left
                buffers.append(pltpu.VMEM((*left, out_rows, width), jnp.float32))
        most = max(counts.values()) - 1
        dma = pltpu.SemaphoreType.DMA
        hbm = pl.BlockSpec(memory_space=pltpu.HBM)
        operands = (
            helper_rack.T,
            helper_node.T,
            helper_block.T,
            coefficients.transpose(1, 2, 3, 0),
            stored.reshape(hold * planes, length),
        )
        buffer_bytes = sum(math.prod(b.shape) * 4 for b in buffers)
        own, came = pl.pallas_call(
            functools.partial(repair_kernel, sizes, groups),
            out_shape=[jax.ShapeDtypeStruct((out_rows, length), jnp.float32)] * 2,
            in_specs=[hbm] * 5,
            out_specs=[pl.BlockSpec(memory_space=pltpu.VMEM)] * 2,
            scratch_shapes=[
                *[pltpu.VMEM(a.shape, a.dtype) for a in operands],
                dma((len(operands),)),
                pltpu.VMEM((2, repairs * planes // CORES, hold * planes), jnp.bfloat16),
                dma((len(groups),)),
                dma((len(groups),)),
                dma((len(tasks), len(counts), most)),
                dma((len(tasks), len(counts), most)),
                *buffers,
            ],
            compiler_params=pltpu.CompilerParams(
                collective_id=0,
                has_side_effects=True,
                vmem_limit_bytes=max(buffer_bytes + 12 * 2**20, 56 * 2**20),
            ),
        )(*operands)
        return (own + came).reshape(-1, planes, length)

    return jax.shard_map(
        on_device,
        mesh=mesh,
        in_specs=(P(("rack", "node"), None, None), P(), P(), P(), P()),
        out_specs=P(("rack", "node"), None, None),
        check_vma=False,
    )
```

```python
import functools
import math

import jax
import jax.numpy as jnp
from jax import lax
from jax.experimental import pallas as pl
from jax.experimental.pallas import tpu as pltpu
from jax.sharding import PartitionSpec as P

MESH = pl.DeviceIdType.MESH
CORES = 2
TILE = 128


def split_z(size):
    axes, stride = [], 1
    while size > 1:
        part = 2 if size % 2 == 0 else size
        axes.append((f"z{len(axes)}", part, stride))
        size, stride = size // part, stride * part
    return axes


def lay_out(length, along_z):
    plane = (("x", "y"), ("y", "x"))
    tiles = length // TILE
    side = tiles * 3 // 16
    widths = []
    left = (tiles - side) // 2
    while left:
        widths.append(min(2, left))
        left -= widths[-1]
    spare = tiles - 2 * sum(widths)
    groups, start = [], 0
    for number, wide in enumerate(widths):
        tasks, at = [], start
        plan = [(order + along_z, wide) for order in plane]
        if spare:
            part = 2 if spare > 2 else 1
            plan.append((along_z + plane[number % 2], part))
            spare -= part
        for order, count in plan:
            tasks.append((order, at * TILE, count * TILE))
            at += count
        groups.append((start * TILE, (at - start) * TILE, tasks))
        start = at
    return groups


def repair_kernel(
    sizes,
    groups,
    rack_hbm,
    node_hbm,
    block_hbm,
    coeffs_hbm,
    stored_hbm,
    out_ref,
    rack_ref,
    node_ref,
    block_ref,
    coeffs_ref,
    stored_ref,
    copy_in,
    weights,
    core_send,
    core_recv,
    task_send,
    task_recv,
    *buffers,
):
    counts, z_axes, helpers, hold, planes, repairs, per_rack = sizes
    ny = counts["y"]
    axes = tuple(counts)
    tasks = [task for group in groups for task in group[2]]
    wide, fetched = buffers[: len(groups)], buffers[len(groups) : 2 * len(groups)]
    held = buffers[2 * len(groups) :]
    depth = len(axes) + 1
    held = [held[depth * t : depth * (t + 1)] for t in range(len(tasks))]

    rack, node = lax.axis_index("rack"), lax.axis_index("node")
    core = lax.rem(rack, CORES)
    place = {"x": lax.div(rack, CORES), "y": lax.rem(node, ny)}
    for name, size, stride in z_axes:
        place[name] = lax.rem(lax.div(node, ny * stride), size)

    def moved(axis, step):
        return lax.rem(place[axis] + step, counts[axis])

    def device(axis, step):
        to = dict(place)
        to[axis] = moved(axis, step)
        z = sum(to[name] * stride for name, _, stride in z_axes)
        return (to["x"] * CORES + core, z * ny + to["y"])

    other_rack = place["x"] * CORES + lax.rem(core + 1, CORES)
    other_core = (other_rack, node)
    peers = [other_core] + [device(a, s) for a in axes for s in range(1, counts[a])]
    barrier = pltpu.get_barrier_semaphore()
    for peer in peers:
        pl.semaphore_signal(barrier, inc=1, device_id=peer, device_id_type=MESH)

    arrays = (
        (rack_hbm, rack_ref),
        (node_hbm, node_ref),
        (block_hbm, block_ref),
        (coeffs_hbm, coeffs_ref),
        (stored_hbm, stored_ref),
    )
    loads = [
        pltpu.make_async_copy(source, target, copy_in.at[i])
        for i, (source, target) in enumerate(arrays)
    ]
    for load in loads:
        load.start()

    def remote(source, target, send, recv, to):
        return pltpu.make_async_remote_copy(
            src_ref=source,
            dst_ref=target,
            send_sem=send,
            recv_sem=recv,
            device_id=to,
            device_id_type=MESH,
        )

    def core_copy(g):
        return remote(wide[g], fetched[g], core_send.at[g], core_recv.at[g], other_core)

    for load in loads[:-1]:
        load.wait()

    here = node_ref[...] == node
    marks = jnp.where(
        here & (rack_ref[...] == rack),
        block_ref[...],
        jnp.where(here & (rack_ref[...] == other_rack), block_ref[...] + hold, -1),
    )
    own_rows = repairs * planes // CORES
    row = lax.broadcasted_iota(jnp.int32, (own_rows, 2 * repairs), 0)
    column = lax.broadcasted_iota(jnp.int32, (own_rows, 2 * repairs), 1)
    row_plane, row_repair = lax.rem(row, planes), lax.div(row, planes)
    row_repair = (
        lax.div(row_repair, per_rack) * CORES + core
    ) * per_rack + lax.rem(row_repair, per_rack)
    hits = row_repair == lax.rem(column, repairs)
    half = planes // 2
    hit_plane = row_plane - lax.div(column, repairs) * half
    marks = jnp.concatenate([marks, marks], axis=1)
    slot = lax.broadcasted_iota(jnp.int32, (2 * hold, planes, 2 * repairs), 0)
    summed = [jnp.zeros((own_rows, hold * planes), jnp.float32)] * 2
    for plane in range(half):
        if plane == half // 2:
            loads[-1].wait()
            for g, (start, width, _) in enumerate(groups):
                piece = stored_ref[:, start : start + width]
                wide[g][...] = piece.astype(jnp.float32)
            pl.semaphore_wait(barrier, len(peers))
            for g in range(len(groups)):
                core_copy(g).start()
        spread = jnp.zeros((2 * hold, planes, 2 * repairs), jnp.float32)
        for helper in range(helpers):
            values = [coeffs_ref[helper, plane + k * half] for k in range(2)]
            values = [value.astype(jnp.float32) for value in values]
            mark = marks[helper : helper + 1, :][None]
            spread = jnp.where(
                slot == mark, jnp.concatenate(values, axis=1)[None], spread
            )
        spread = spread.reshape(2 * hold * planes, 2 * repairs).astype(jnp.bfloat16)
        picked = (hits & (hit_plane == plane)).astype(jnp.float32).astype(jnp.bfloat16)
        for part in range(2):
            summed[part] += lax.dot_general(
                picked,
                spread[part * hold * planes : (part + 1) * hold * planes],
                (((1,), (1,)), ((), ())),
                preferred_element_type=jnp.float32,
            )
    for part in range(2):
        weights[part] = summed[part].astype(jnp.bfloat16)

    def before(t, stage):
        order = tasks[t][0]
        left = [axis for axis in axes if axis not in order[:stage]]
        ahead = (slice(None),) * left.index(order[stage])
        if stage == 0:
            return held[t][0], lambda at: ahead + (at,)
        return held[t][stage], lambda at: (0,) + ahead + (at,)

    def copies(t, stage):
        axis = tasks[t][0][stage]
        source, pick = before(t, stage)
        return [
            remote(
                source.at[pick(moved(axis, s))],
                held[t][stage + 1].at[s - 1],
                task_send.at[t, stage, s - 1],
                task_recv.at[t, stage, s - 1],
                device(axis, s),
            )
            for s in range(1, counts[axis])
        ]

    def gathered(t, stage):
        axis = tasks[t][0][stage]
        source, pick = before(t, stage)
        arrived = copies(t, stage)
        for copy in arrived:
            copy.wait_recv()
        came = held[t][stage + 1][0]
        for s in range(1, len(arrived)):
            came += held[t][stage + 1][s]
        return source[pick(place[axis])], came

    def begin(g):
        start, width, inside = groups[g]
        core_copy(g).wait_recv()
        near = stored_ref[:, start : start + width]
        far = fetched[g][...].astype(jnp.bfloat16)
        total = jnp.dot(weights[0], near, preferred_element_type=jnp.float32)
        total += jnp.dot(weights[1], far, preferred_element_type=jnp.float32)
        for t in members[g]:
            _, at, count = tasks[t]
            piece = total[:, at - start : at - start + count]
            held[t][0][...] = piece.reshape(held[t][0].shape)
            for copy in copies(t, 0):
                copy.start()

    def advance(g, stage):
        for t in members[g]:
            own, came = gathered(t, stage - 1)
            held[t][stage][0] = own + came
            for copy in copies(t, stage):
                copy.start()

    def finish(g):
        for t in members[g]:
            _, at, count = tasks[t]
            own, came = gathered(t, len(axes) - 1)
            out_ref[:, at : at + count] = own + came

    members, seen = [], 0
    for _, _, inside in groups:
        members.append(range(seen, seen + len(inside)))
        seen += len(inside)
    steps = (
        begin,
        *[functools.partial(advance, stage=stage) for stage in range(1, len(axes))],
        finish,
    )
    delays = (0, *range(2, len(axes) + 1), len(axes) + 4)
    for tick in range(len(groups) + delays[-1]):
        for delay, step in zip(delays, steps):
            if 0 <= tick - delay < len(groups):
                step(tick - delay)

    for g in range(len(groups)):
        core_copy(g).wait_send()
        for t in members[g]:
            for stage in range(len(axes)):
                for copy in copies(t, stage):
                    copy.wait_send()


def solution(mesh):
    racks, nodes = mesh.shape["rack"], mesh.shape["node"]
    z_axes = split_z(nodes // 2)
    counts = {"x": racks // CORES}
    counts.update({name: size for name, size, _ in reversed(z_axes)})
    counts["y"] = 2

    def on_device(stored, coefficients, helper_rack, helper_node, helper_block):
        hold, planes, length = stored.shape
        repairs, helpers = helper_block.shape
        out_rows = repairs // (racks * nodes) * planes
        groups = lay_out(length, tuple(name for name, _, _ in z_axes))
        tasks = [task for group in groups for task in group[2]]
        sizes = (counts, z_axes, helpers, hold, planes, repairs, repairs // racks)
        buffers = [
            pltpu.VMEM((hold * planes, width), jnp.float32)
            for _ in range(2)
            for _, width, _ in groups
        ]
        for order, _, width in tasks:
            for stage in range(len(counts) + 1):
                left = [counts[a] for a in counts if a not in order[:stage]]
                if stage:
                    left = [counts[order[stage - 1]] - 1] + left
                buffers.append(pltpu.VMEM((*left, out_rows, width), jnp.float32))
        most = max(counts.values()) - 1
        dma = pltpu.SemaphoreType.DMA
        hbm = pl.BlockSpec(memory_space=pltpu.HBM)
        operands = (
            helper_rack.T,
            helper_node.T,
            helper_block.T,
            coefficients.transpose(1, 2, 3, 0),
            stored.reshape(hold * planes, length),
        )
        buffer_bytes = sum(math.prod(b.shape) * 4 for b in buffers)
        rebuilt = pl.pallas_call(
            functools.partial(repair_kernel, sizes, groups),
            out_shape=jax.ShapeDtypeStruct((out_rows, length), jnp.float32),
            in_specs=[hbm] * 5,
            out_specs=pl.BlockSpec(memory_space=pltpu.VMEM),
            scratch_shapes=[
                *[pltpu.VMEM(a.shape, a.dtype) for a in operands],
                dma((len(operands),)),
                pltpu.VMEM((2, repairs * planes // CORES, hold * planes), jnp.bfloat16),
                dma((len(groups),)),
                dma((len(groups),)),
                dma((len(tasks), len(counts), most)),
                dma((len(tasks), len(counts), most)),
                *buffers,
            ],
            compiler_params=pltpu.CompilerParams(
                collective_id=0,
                has_side_effects=True,
                vmem_limit_bytes=max(buffer_bytes + 12 * 2**20, 56 * 2**20),
            ),
        )(*operands)
        return rebuilt.reshape(-1, planes, length)

    return jax.shard_map(
        on_device,
        mesh=mesh,
        in_specs=(P(("rack", "node"), None, None), P(), P(), P(), P()),
        out_specs=P(("rack", "node"), None, None),
        check_vma=False,
    )
```

```python
import functools
import math

import jax
import jax.numpy as jnp
from jax import lax
from jax.experimental import pallas as pl
from jax.experimental.pallas import tpu as pltpu
from jax.sharding import PartitionSpec as P

MESH = pl.DeviceIdType.MESH
CORES = 2
TILE = 128


def split_z(size):
    axes, stride = [], 1
    while size > 1:
        part = 2 if size % 2 == 0 else size
        axes.append((f"z{len(axes)}", part, stride))
        size, stride = size // part, stride * part
    return axes


def lay_out(length, along_z):
    plane = (("x", "y"), ("y", "x"))
    tiles = length // TILE
    side = tiles // 4
    widths = []
    left = (tiles - side) // 2
    while left:
        widths.append(min(2, left))
        left -= widths[-1]
    spare = tiles - 2 * sum(widths)
    groups, start = [], 0
    for number, wide in enumerate(widths):
        tasks, at = [], start
        plan = [(order + along_z, wide) for order in plane]
        if spare:
            part = -(-spare // (len(widths) - number))
            plan.append((along_z + plane[number % 2], part))
            spare -= part
        for order, count in plan:
            tasks.append((order, at * TILE, count * TILE))
            at += count
        groups.append((start * TILE, (at - start) * TILE, tasks))
        start = at
    return groups


def repair_kernel(
    sizes,
    groups,
    rack_hbm,
    node_hbm,
    block_hbm,
    coeffs_hbm,
    stored_hbm,
    out_ref,
    rack_ref,
    node_ref,
    block_ref,
    coeffs_ref,
    stored_ref,
    copy_in,
    weights,
    core_send,
    core_recv,
    task_send,
    task_recv,
    *buffers,
):
    counts, z_axes, helpers, hold, planes, repairs, per_rack = sizes
    ny = counts["y"]
    axes = tuple(counts)
    tasks = [task for group in groups for task in group[2]]
    wide, fetched = buffers[: len(groups)], buffers[len(groups) : 2 * len(groups)]
    held = buffers[2 * len(groups) :]
    depth = len(axes) + 1
    held = [held[depth * t : depth * (t + 1)] for t in range(len(tasks))]

    rack, node = lax.axis_index("rack"), lax.axis_index("node")
    core = lax.rem(rack, CORES)
    place = {"x": lax.div(rack, CORES), "y": lax.rem(node, ny)}
    for name, size, stride in z_axes:
        place[name] = lax.rem(lax.div(node, ny * stride), size)

    def moved(axis, step):
        return lax.rem(place[axis] + step, counts[axis])

    def device(axis, step):
        to = dict(place)
        to[axis] = moved(axis, step)
        z = sum(to[name] * stride for name, _, stride in z_axes)
        return (to["x"] * CORES + core, z * ny + to["y"])

    other_rack = place["x"] * CORES + lax.rem(core + 1, CORES)
    other_core = (other_rack, node)
    peers = [other_core] + [device(a, s) for a in axes for s in range(1, counts[a])]
    barrier = pltpu.get_barrier_semaphore()
    for peer in peers:
        pl.semaphore_signal(barrier, inc=1, device_id=peer, device_id_type=MESH)

    arrays = (
        (rack_hbm, rack_ref),
        (node_hbm, node_ref),
        (block_hbm, block_ref),
        (coeffs_hbm, coeffs_ref),
        (stored_hbm, stored_ref),
    )
    loads = [
        pltpu.make_async_copy(source, target, copy_in.at[i])
        for i, (source, target) in enumerate(arrays)
    ]
    for load in loads:
        load.start()

    def remote(source, target, send, recv, to):
        return pltpu.make_async_remote_copy(
            src_ref=source,
            dst_ref=target,
            send_sem=send,
            recv_sem=recv,
            device_id=to,
            device_id_type=MESH,
        )

    def core_copy(g):
        return remote(wide[g], fetched[g], core_send.at[g], core_recv.at[g], other_core)

    for load in loads[:-1]:
        load.wait()

    here = node_ref[...] == node
    marks = jnp.where(
        here & (rack_ref[...] == rack),
        block_ref[...],
        jnp.where(here & (rack_ref[...] == other_rack), block_ref[...] + hold, -1),
    )
    own_rows = repairs * planes // CORES
    row = lax.broadcasted_iota(jnp.int32, (own_rows, 2 * repairs), 0)
    column = lax.broadcasted_iota(jnp.int32, (own_rows, 2 * repairs), 1)
    row_plane, row_repair = lax.rem(row, planes), lax.div(row, planes)
    row_repair = (
        lax.div(row_repair, per_rack) * CORES + core
    ) * per_rack + lax.rem(row_repair, per_rack)
    hits = row_repair == lax.rem(column, repairs)
    half = planes // 2
    hit_plane = row_plane - lax.div(column, repairs) * half
    marks = jnp.concatenate([marks, marks], axis=1)
    slot = lax.broadcasted_iota(jnp.int32, (2 * hold, planes, 2 * repairs), 0)
    summed = [jnp.zeros((own_rows, hold * planes), jnp.float32)] * 2
    for plane in range(half):
        if plane == half // 2:
            loads[-1].wait()
            for g, (start, width, _) in enumerate(groups):
                piece = stored_ref[:, start : start + width]
                wide[g][...] = piece.astype(jnp.float32)
            pl.semaphore_wait(barrier, len(peers))
            for g in range(len(groups)):
                core_copy(g).start()
        spread = jnp.zeros((2 * hold, planes, 2 * repairs), jnp.float32)
        for helper in range(helpers):
            values = [coeffs_ref[helper, plane + k * half] for k in range(2)]
            values = [value.astype(jnp.float32) for value in values]
            mark = marks[helper : helper + 1, :][None]
            spread = jnp.where(
                slot == mark, jnp.concatenate(values, axis=1)[None], spread
            )
        spread = spread.reshape(2 * hold * planes, 2 * repairs).astype(jnp.bfloat16)
        picked = (hits & (hit_plane == plane)).astype(jnp.float32).astype(jnp.bfloat16)
        for part in range(2):
            summed[part] += lax.dot_general(
                picked,
                spread[part * hold * planes : (part + 1) * hold * planes],
                (((1,), (1,)), ((), ())),
                preferred_element_type=jnp.float32,
            )
    for part in range(2):
        weights[part] = summed[part].astype(jnp.bfloat16)

    def before(t, stage):
        order = tasks[t][0]
        left = [axis for axis in axes if axis not in order[:stage]]
        ahead = (slice(None),) * left.index(order[stage])
        if stage == 0:
            return held[t][0], lambda at: ahead + (at,)
        return held[t][stage], lambda at: (0,) + ahead + (at,)

    def copies(t, stage):
        axis = tasks[t][0][stage]
        source, pick = before(t, stage)
        return [
            remote(
                source.at[pick(moved(axis, s))],
                held[t][stage + 1].at[s - 1],
                task_send.at[t, stage, s - 1],
                task_recv.at[t, stage, s - 1],
                device(axis, s),
            )
            for s in range(1, counts[axis])
        ]

    def gathered(t, stage):
        axis = tasks[t][0][stage]
        source, pick = before(t, stage)
        arrived = copies(t, stage)
        for copy in arrived:
            copy.wait_recv()
        came = held[t][stage + 1][0]
        for s in range(1, len(arrived)):
            came += held[t][stage + 1][s]
        return source[pick(place[axis])], came

    def begin(g):
        start, width, inside = groups[g]
        core_copy(g).wait_recv()
        near = stored_ref[:, start : start + width]
        far = fetched[g][...].astype(jnp.bfloat16)
        total = jnp.dot(weights[0], near, preferred_element_type=jnp.float32)
        total += jnp.dot(weights[1], far, preferred_element_type=jnp.float32)
        for t in members[g]:
            _, at, count = tasks[t]
            piece = total[:, at - start : at - start + count]
            held[t][0][...] = piece.reshape(held[t][0].shape)
            for copy in copies(t, 0):
                copy.start()

    def advance(g, stage):
        for t in members[g]:
            own, came = gathered(t, stage - 1)
            held[t][stage][0] = own + came
            for copy in copies(t, stage):
                copy.start()

    def finish(g):
        for t in members[g]:
            _, at, count = tasks[t]
            own, came = gathered(t, len(axes) - 1)
            out_ref[:, at : at + count] = own + came

    members, seen = [], 0
    for _, _, inside in groups:
        members.append(range(seen, seen + len(inside)))
        seen += len(inside)
    steps = (
        begin,
        *[functools.partial(advance, stage=stage) for stage in range(1, len(axes))],
        finish,
    )
    delays = (*range(len(axes)), len(axes) + 3)
    for tick in range(len(groups) + delays[-1]):
        for delay, step in zip(delays, steps):
            if 0 <= tick - delay < len(groups):
                step(tick - delay)

    for g in range(len(groups)):
        core_copy(g).wait_send()
        for t in members[g]:
            for stage in range(len(axes)):
                for copy in copies(t, stage):
                    copy.wait_send()


def solution(mesh):
    racks, nodes = mesh.shape["rack"], mesh.shape["node"]
    z_axes = split_z(nodes // 2)
    counts = {"x": racks // CORES}
    counts.update({name: size for name, size, _ in reversed(z_axes)})
    counts["y"] = 2

    def on_device(stored, coefficients, helper_rack, helper_node, helper_block):
        hold, planes, length = stored.shape
        repairs, helpers = helper_block.shape
        out_rows = repairs // (racks * nodes) * planes
        groups = lay_out(length, tuple(name for name, _, _ in z_axes))
        tasks = [task for group in groups for task in group[2]]
        sizes = (counts, z_axes, helpers, hold, planes, repairs, repairs // racks)
        buffers = [
            pltpu.VMEM((hold * planes, width), jnp.float32)
            for _ in range(2)
            for _, width, _ in groups
        ]
        for order, _, width in tasks:
            for stage in range(len(counts) + 1):
                left = [counts[a] for a in counts if a not in order[:stage]]
                if stage:
                    left = [counts[order[stage - 1]] - 1] + left
                buffers.append(pltpu.VMEM((*left, out_rows, width), jnp.float32))
        most = max(counts.values()) - 1
        dma = pltpu.SemaphoreType.DMA
        hbm = pl.BlockSpec(memory_space=pltpu.HBM)
        operands = (
            helper_rack.T,
            helper_node.T,
            helper_block.T,
            coefficients.transpose(1, 2, 3, 0),
            stored.reshape(hold * planes, length),
        )
        buffer_bytes = sum(math.prod(b.shape) * 4 for b in buffers)
        rebuilt = pl.pallas_call(
            functools.partial(repair_kernel, sizes, groups),
            out_shape=jax.ShapeDtypeStruct((out_rows, length), jnp.float32),
            in_specs=[hbm] * 5,
            out_specs=pl.BlockSpec(memory_space=pltpu.VMEM),
            scratch_shapes=[
                *[pltpu.VMEM(a.shape, a.dtype) for a in operands],
                dma((len(operands),)),
                pltpu.VMEM((2, repairs * planes // CORES, hold * planes), jnp.bfloat16),
                dma((len(groups),)),
                dma((len(groups),)),
                dma((len(tasks), len(counts), most)),
                dma((len(tasks), len(counts), most)),
                *buffers,
            ],
            compiler_params=pltpu.CompilerParams(
                collective_id=0,
                has_side_effects=True,
                vmem_limit_bytes=max(buffer_bytes + 12 * 2**20, 56 * 2**20),
            ),
        )(*operands)
        return rebuilt.reshape(-1, planes, length)

    return jax.shard_map(
        on_device,
        mesh=mesh,
        in_specs=(P(("rack", "node"), None, None), P(), P(), P(), P()),
        out_specs=P(("rack", "node"), None, None),
        check_vma=False,
    )
```

```python
import functools
import math

import jax
import jax.numpy as jnp
from jax import lax
from jax.experimental import pallas as pl
from jax.experimental.pallas import tpu as pltpu
from jax.sharding import PartitionSpec as P

MESH = pl.DeviceIdType.MESH
CORES = 2
TILE = 128


def split_z(size):
    axes, stride = [], 1
    while size > 1:
        part = 2 if size % 2 == 0 else size
        axes.append((f"z{len(axes)}", part, stride))
        size, stride = size // part, stride * part
    return axes


def lay_out(length, along_z):
    plane = (("x", "y"), ("y", "x"))
    tiles = length // TILE
    side = tiles * 3 // 8
    widths = []
    left = (tiles - side) // 2
    while left:
        widths.append(min(2, left))
        left -= widths[-1]
    spare = tiles - 2 * sum(widths)
    groups, start = [], 0
    for number, wide in enumerate(widths):
        tasks, at = [], start
        plan = [(order + along_z, wide) for order in plane]
        if spare:
            part = -(-spare // (len(widths) - number))
            plan.append((along_z + plane[number % 2], part))
            spare -= part
        for order, count in plan:
            tasks.append((order, at * TILE, count * TILE))
            at += count
        groups.append((start * TILE, (at - start) * TILE, tasks))
        start = at
    return groups


def repair_kernel(
    sizes,
    groups,
    rack_hbm,
    node_hbm,
    block_hbm,
    coeffs_hbm,
    stored_hbm,
    out_ref,
    rack_ref,
    node_ref,
    block_ref,
    coeffs_ref,
    stored_ref,
    copy_in,
    weights,
    core_send,
    core_recv,
    task_send,
    task_recv,
    *buffers,
):
    counts, z_axes, helpers, hold, planes, repairs, per_rack = sizes
    ny = counts["y"]
    axes = tuple(counts)
    tasks = [task for group in groups for task in group[2]]
    wide, fetched = buffers[: len(groups)], buffers[len(groups) : 2 * len(groups)]
    held = buffers[2 * len(groups) :]
    depth = len(axes) + 1
    held = [held[depth * t : depth * (t + 1)] for t in range(len(tasks))]

    rack, node = lax.axis_index("rack"), lax.axis_index("node")
    core = lax.rem(rack, CORES)
    place = {"x": lax.div(rack, CORES), "y": lax.rem(node, ny)}
    for name, size, stride in z_axes:
        place[name] = lax.rem(lax.div(node, ny * stride), size)

    def moved(axis, step):
        return lax.rem(place[axis] + step, counts[axis])

    def device(axis, step):
        to = dict(place)
        to[axis] = moved(axis, step)
        z = sum(to[name] * stride for name, _, stride in z_axes)
        return (to["x"] * CORES + core, z * ny + to["y"])

    other_rack = place["x"] * CORES + lax.rem(core + 1, CORES)
    other_core = (other_rack, node)
    peers = [other_core] + [device(a, s) for a in axes for s in range(1, counts[a])]
    barrier = pltpu.get_barrier_semaphore()
    for peer in peers:
        pl.semaphore_signal(barrier, inc=1, device_id=peer, device_id_type=MESH)

    arrays = (
        (rack_hbm, rack_ref),
        (node_hbm, node_ref),
        (block_hbm, block_ref),
        (coeffs_hbm, coeffs_ref),
        (stored_hbm, stored_ref),
    )
    loads = [
        pltpu.make_async_copy(source, target, copy_in.at[i])
        for i, (source, target) in enumerate(arrays)
    ]
    for load in loads:
        load.start()

    def remote(source, target, send, recv, to):
        return pltpu.make_async_remote_copy(
            src_ref=source,
            dst_ref=target,
            send_sem=send,
            recv_sem=recv,
            device_id=to,
            device_id_type=MESH,
        )

    def core_copy(g):
        return remote(wide[g], fetched[g], core_send.at[g], core_recv.at[g], other_core)

    for load in loads[:-1]:
        load.wait()

    here = node_ref[...] == node
    marks = jnp.where(
        here & (rack_ref[...] == rack),
        block_ref[...],
        jnp.where(here & (rack_ref[...] == other_rack), block_ref[...] + hold, -1),
    )
    own_rows = repairs * planes // CORES
    row = lax.broadcasted_iota(jnp.int32, (own_rows, 2 * repairs), 0)
    column = lax.broadcasted_iota(jnp.int32, (own_rows, 2 * repairs), 1)
    row_plane, row_repair = lax.rem(row, planes), lax.div(row, planes)
    row_repair = (
        lax.div(row_repair, per_rack) * CORES + core
    ) * per_rack + lax.rem(row_repair, per_rack)
    hits = row_repair == lax.rem(column, repairs)
    half = planes // 2
    hit_plane = row_plane - lax.div(column, repairs) * half
    marks = jnp.concatenate([marks, marks], axis=1)
    slot = lax.broadcasted_iota(jnp.int32, (2 * hold, planes, 2 * repairs), 0)
    summed = [jnp.zeros((own_rows, hold * planes), jnp.float32)] * 2
    for plane in range(half):
        if plane == half // 2:
            loads[-1].wait()
            for g, (start, width, _) in enumerate(groups):
                piece = stored_ref[:, start : start + width]
                wide[g][...] = piece.astype(jnp.float32)
            pl.semaphore_wait(barrier, len(peers))
            for g in range(len(groups)):
                core_copy(g).start()
        spread = jnp.zeros((2 * hold, planes, 2 * repairs), jnp.float32)
        for helper in range(helpers):
            values = [coeffs_ref[helper, plane + k * half] for k in range(2)]
            values = [value.astype(jnp.float32) for value in values]
            mark = marks[helper : helper + 1, :][None]
            spread = jnp.where(
                slot == mark, jnp.concatenate(values, axis=1)[None], spread
            )
        spread = spread.reshape(2 * hold * planes, 2 * repairs).astype(jnp.bfloat16)
        picked = (hits & (hit_plane == plane)).astype(jnp.float32).astype(jnp.bfloat16)
        for part in range(2):
            summed[part] += lax.dot_general(
                picked,
                spread[part * hold * planes : (part + 1) * hold * planes],
                (((1,), (1,)), ((), ())),
                preferred_element_type=jnp.float32,
            )
    for part in range(2):
        weights[part] = summed[part].astype(jnp.bfloat16)

    def before(t, stage):
        order = tasks[t][0]
        left = [axis for axis in axes if axis not in order[:stage]]
        ahead = (slice(None),) * left.index(order[stage])
        if stage == 0:
            return held[t][0], lambda at: ahead + (at,)
        return held[t][stage], lambda at: (0,) + ahead + (at,)

    def copies(t, stage):
        axis = tasks[t][0][stage]
        source, pick = before(t, stage)
        return [
            remote(
                source.at[pick(moved(axis, s))],
                held[t][stage + 1].at[s - 1],
                task_send.at[t, stage, s - 1],
                task_recv.at[t, stage, s - 1],
                device(axis, s),
            )
            for s in range(1, counts[axis])
        ]

    def gathered(t, stage):
        axis = tasks[t][0][stage]
        source, pick = before(t, stage)
        arrived = copies(t, stage)
        for copy in arrived:
            copy.wait_recv()
        came = held[t][stage + 1][0]
        for s in range(1, len(arrived)):
            came += held[t][stage + 1][s]
        return source[pick(place[axis])], came

    def begin(g):
        start, width, inside = groups[g]
        core_copy(g).wait_recv()
        near = stored_ref[:, start : start + width]
        far = fetched[g][...].astype(jnp.bfloat16)
        total = jnp.dot(weights[0], near, preferred_element_type=jnp.float32)
        total += jnp.dot(weights[1], far, preferred_element_type=jnp.float32)
        for t in members[g]:
            _, at, count = tasks[t]
            piece = total[:, at - start : at - start + count]
            held[t][0][...] = piece.reshape(held[t][0].shape)
            for copy in copies(t, 0):
                copy.start()

    def advance(g, stage):
        for t in members[g]:
            own, came = gathered(t, stage - 1)
            held[t][stage][0] = own + came
            for copy in copies(t, stage):
                copy.start()

    def finish(g):
        for t in members[g]:
            _, at, count = tasks[t]
            own, came = gathered(t, len(axes) - 1)
            out_ref[:, at : at + count] = own + came

    members, seen = [], 0
    for _, _, inside in groups:
        members.append(range(seen, seen + len(inside)))
        seen += len(inside)
    steps = (
        begin,
        *[functools.partial(advance, stage=stage) for stage in range(1, len(axes))],
        finish,
    )
    delays = (*range(len(axes)), len(axes) + 3)
    for tick in range(len(groups) + delays[-1]):
        for delay, step in zip(delays, steps):
            if 0 <= tick - delay < len(groups):
                step(tick - delay)

    for g in range(len(groups)):
        core_copy(g).wait_send()
        for t in members[g]:
            for stage in range(len(axes)):
                for copy in copies(t, stage):
                    copy.wait_send()


def solution(mesh):
    racks, nodes = mesh.shape["rack"], mesh.shape["node"]
    z_axes = split_z(nodes // 2)
    counts = {"x": racks // CORES}
    counts.update({name: size for name, size, _ in reversed(z_axes)})
    counts["y"] = 2

    def on_device(stored, coefficients, helper_rack, helper_node, helper_block):
        hold, planes, length = stored.shape
        repairs, helpers = helper_block.shape
        out_rows = repairs // (racks * nodes) * planes
        groups = lay_out(length, tuple(name for name, _, _ in z_axes))
        tasks = [task for group in groups for task in group[2]]
        sizes = (counts, z_axes, helpers, hold, planes, repairs, repairs // racks)
        buffers = [
            pltpu.VMEM((hold * planes, width), jnp.float32)
            for _ in range(2)
            for _, width, _ in groups
        ]
        for order, _, width in tasks:
            for stage in range(len(counts) + 1):
                left = [counts[a] for a in counts if a not in order[:stage]]
                if stage:
                    left = [counts[order[stage - 1]] - 1] + left
                buffers.append(pltpu.VMEM((*left, out_rows, width), jnp.float32))
        most = max(counts.values()) - 1
        dma = pltpu.SemaphoreType.DMA
        hbm = pl.BlockSpec(memory_space=pltpu.HBM)
        operands = (
            helper_rack.T,
            helper_node.T,
            helper_block.T,
            coefficients.transpose(1, 2, 3, 0),
            stored.reshape(hold * planes, length),
        )
        buffer_bytes = sum(math.prod(b.shape) * 4 for b in buffers)
        rebuilt = pl.pallas_call(
            functools.partial(repair_kernel, sizes, groups),
            out_shape=jax.ShapeDtypeStruct((out_rows, length), jnp.float32),
            in_specs=[hbm] * 5,
            out_specs=pl.BlockSpec(memory_space=pltpu.VMEM),
            scratch_shapes=[
                *[pltpu.VMEM(a.shape, a.dtype) for a in operands],
                dma((len(operands),)),
                pltpu.VMEM((2, repairs * planes // CORES, hold * planes), jnp.bfloat16),
                dma((len(groups),)),
                dma((len(groups),)),
                dma((len(tasks), len(counts), most)),
                dma((len(tasks), len(counts), most)),
                *buffers,
            ],
            compiler_params=pltpu.CompilerParams(
                collective_id=0,
                has_side_effects=True,
                vmem_limit_bytes=max(buffer_bytes + 12 * 2**20, 56 * 2**20),
            ),
        )(*operands)
        return rebuilt.reshape(-1, planes, length)

    return jax.shard_map(
        on_device,
        mesh=mesh,
        in_specs=(P(("rack", "node"), None, None), P(), P(), P(), P()),
        out_specs=P(("rack", "node"), None, None),
        check_vma=False,
    )
```

```python
import functools
import math

import jax
import jax.numpy as jnp
from jax import lax
from jax.experimental import pallas as pl
from jax.experimental.pallas import tpu as pltpu
from jax.sharding import PartitionSpec as P

MESH = pl.DeviceIdType.MESH
CORES = 2
TILE = 128


def split_z(size):
    axes, stride = [], 1
    while size > 1:
        part = 2 if size % 2 == 0 else size
        axes.append((f"z{len(axes)}", part, stride))
        size, stride = size // part, stride * part
    return axes


def lay_out(length, along_z):
    plane = (("x", "y"), ("y", "x"))
    tiles = length // TILE
    side = tiles // 4
    widths = []
    left = (tiles - side) // 2
    while left:
        widths.append(min(2, left))
        left -= widths[-1]
    spare = tiles - 2 * sum(widths)
    groups, start = [], 0
    for number, wide in enumerate(widths):
        tasks, at = [], start
        plan = [(order + along_z, wide) for order in plane]
        if spare:
            part = min(2, spare)
            plan.append((along_z + plane[number % 2], part))
            spare -= part
        for order, count in plan:
            tasks.append((order, at * TILE, count * TILE))
            at += count
        groups.append((start * TILE, (at - start) * TILE, tasks))
        start = at
    return groups


def repair_kernel(
    sizes,
    groups,
    rack_hbm,
    node_hbm,
    block_hbm,
    coeffs_hbm,
    stored_hbm,
    out_ref,
    rack_ref,
    node_ref,
    block_ref,
    coeffs_ref,
    stored_ref,
    copy_in,
    weights,
    core_send,
    core_recv,
    task_send,
    task_recv,
    *buffers,
):
    counts, z_axes, helpers, hold, planes, repairs, per_rack = sizes
    ny = counts["y"]
    axes = tuple(counts)
    tasks = [task for group in groups for task in group[2]]
    wide, fetched = buffers[: len(groups)], buffers[len(groups) : 2 * len(groups)]
    held = buffers[2 * len(groups) :]
    depth = len(axes) + 1
    held = [held[depth * t : depth * (t + 1)] for t in range(len(tasks))]

    rack, node = lax.axis_index("rack"), lax.axis_index("node")
    core = lax.rem(rack, CORES)
    place = {"x": lax.div(rack, CORES), "y": lax.rem(node, ny)}
    for name, size, stride in z_axes:
        place[name] = lax.rem(lax.div(node, ny * stride), size)

    def moved(axis, step):
        return lax.rem(place[axis] + step, counts[axis])

    def device(axis, step):
        to = dict(place)
        to[axis] = moved(axis, step)
        z = sum(to[name] * stride for name, _, stride in z_axes)
        return (to["x"] * CORES + core, z * ny + to["y"])

    other_rack = place["x"] * CORES + lax.rem(core + 1, CORES)
    other_core = (other_rack, node)
    peers = [other_core] + [device(a, s) for a in axes for s in range(1, counts[a])]
    barrier = pltpu.get_barrier_semaphore()
    for peer in peers:
        pl.semaphore_signal(barrier, inc=1, device_id=peer, device_id_type=MESH)

    arrays = (
        (rack_hbm, rack_ref),
        (node_hbm, node_ref),
        (block_hbm, block_ref),
        (coeffs_hbm, coeffs_ref),
        (stored_hbm, stored_ref),
    )
    loads = [
        pltpu.make_async_copy(source, target, copy_in.at[i])
        for i, (source, target) in enumerate(arrays)
    ]
    for load in loads:
        load.start()

    def remote(source, target, send, recv, to):
        return pltpu.make_async_remote_copy(
            src_ref=source,
            dst_ref=target,
            send_sem=send,
            recv_sem=recv,
            device_id=to,
            device_id_type=MESH,
        )

    def core_copy(g):
        return remote(wide[g], fetched[g], core_send.at[g], core_recv.at[g], other_core)

    for load in loads[:-1]:
        load.wait()

    here = node_ref[...] == node
    marks = jnp.where(
        here & (rack_ref[...] == rack),
        block_ref[...],
        jnp.where(here & (rack_ref[...] == other_rack), block_ref[...] + hold, -1),
    )
    own_rows = repairs * planes // CORES
    row = lax.broadcasted_iota(jnp.int32, (own_rows, 2 * repairs), 0)
    column = lax.broadcasted_iota(jnp.int32, (own_rows, 2 * repairs), 1)
    row_plane, row_repair = lax.rem(row, planes), lax.div(row, planes)
    row_repair = (
        lax.div(row_repair, per_rack) * CORES + core
    ) * per_rack + lax.rem(row_repair, per_rack)
    hits = row_repair == lax.rem(column, repairs)
    half = planes // 2
    hit_plane = row_plane - lax.div(column, repairs) * half
    marks = jnp.concatenate([marks, marks], axis=1)
    slot = lax.broadcasted_iota(jnp.int32, (2 * hold, planes, 2 * repairs), 0)
    summed = [jnp.zeros((own_rows, hold * planes), jnp.float32)] * 2
    for plane in range(half):
        if plane == half // 2:
            loads[-1].wait()
            for g, (start, width, _) in enumerate(groups):
                piece = stored_ref[:, start : start + width]
                wide[g][...] = piece.astype(jnp.float32)
            pl.semaphore_wait(barrier, len(peers))
            for g in range(len(groups)):
                core_copy(g).start()
        spread = jnp.zeros((2 * hold, planes, 2 * repairs), jnp.float32)
        for helper in range(helpers):
            values = [coeffs_ref[helper, plane + k * half] for k in range(2)]
            values = [value.astype(jnp.float32) for value in values]
            mark = marks[helper : helper + 1, :][None]
            spread = jnp.where(
                slot == mark, jnp.concatenate(values, axis=1)[None], spread
            )
        spread = spread.reshape(2 * hold * planes, 2 * repairs).astype(jnp.bfloat16)
        picked = (hits & (hit_plane == plane)).astype(jnp.float32).astype(jnp.bfloat16)
        for part in range(2):
            summed[part] += lax.dot_general(
                picked,
                spread[part * hold * planes : (part + 1) * hold * planes],
                (((1,), (1,)), ((), ())),
                preferred_element_type=jnp.float32,
            )
    for part in range(2):
        weights[part] = summed[part].astype(jnp.bfloat16)

    def before(t, stage):
        order = tasks[t][0]
        left = [axis for axis in axes if axis not in order[:stage]]
        ahead = (slice(None),) * left.index(order[stage])
        if stage == 0:
            return held[t][0], lambda at: ahead + (at,)
        return held[t][stage], lambda at: (0,) + ahead + (at,)

    def copies(t, stage):
        axis = tasks[t][0][stage]
        source, pick = before(t, stage)
        return [
            remote(
                source.at[pick(moved(axis, s))],
                held[t][stage + 1].at[s - 1],
                task_send.at[t, stage, s - 1],
                task_recv.at[t, stage, s - 1],
                device(axis, s),
            )
            for s in range(1, counts[axis])
        ]

    def gathered(t, stage):
        axis = tasks[t][0][stage]
        source, pick = before(t, stage)
        arrived = copies(t, stage)
        for copy in arrived:
            copy.wait_recv()
        came = held[t][stage + 1][0]
        for s in range(1, len(arrived)):
            came += held[t][stage + 1][s]
        return source[pick(place[axis])], came

    def begin(g):
        start, width, inside = groups[g]
        core_copy(g).wait_recv()
        near = stored_ref[:, start : start + width]
        far = fetched[g][...].astype(jnp.bfloat16)
        total = jnp.dot(weights[0], near, preferred_element_type=jnp.float32)
        total += jnp.dot(weights[1], far, preferred_element_type=jnp.float32)
        for t in members[g]:
            _, at, count = tasks[t]
            piece = total[:, at - start : at - start + count]
            held[t][0][...] = piece.reshape(held[t][0].shape)
            for copy in copies(t, 0):
                copy.start()

    def advance(g, stage):
        for t in members[g]:
            own, came = gathered(t, stage - 1)
            held[t][stage][0] = own + came
            for copy in copies(t, stage):
                copy.start()

    def finish(g):
        for t in members[g]:
            _, at, count = tasks[t]
            own, came = gathered(t, len(axes) - 1)
            out_ref[:, at : at + count] = own + came

    members, seen = [], 0
    for _, _, inside in groups:
        members.append(range(seen, seen + len(inside)))
        seen += len(inside)
    steps = (
        begin,
        *[functools.partial(advance, stage=stage) for stage in range(1, len(axes))],
        finish,
    )
    delays = (*range(len(axes)), len(axes) + 3)
    for tick in range(len(groups) + delays[-1]):
        for delay, step in zip(delays, steps):
            if 0 <= tick - delay < len(groups):
                step(tick - delay)

    for g in range(len(groups)):
        core_copy(g).wait_send()
        for t in members[g]:
            for stage in range(len(axes)):
                for copy in copies(t, stage):
                    copy.wait_send()


def solution(mesh):
    racks, nodes = mesh.shape["rack"], mesh.shape["node"]
    z_axes = split_z(nodes // 2)
    counts = {"x": racks // CORES}
    counts.update({name: size for name, size, _ in reversed(z_axes)})
    counts["y"] = 2

    def on_device(stored, coefficients, helper_rack, helper_node, helper_block):
        hold, planes, length = stored.shape
        repairs, helpers = helper_block.shape
        out_rows = repairs // (racks * nodes) * planes
        groups = lay_out(length, tuple(name for name, _, _ in z_axes))
        tasks = [task for group in groups for task in group[2]]
        sizes = (counts, z_axes, helpers, hold, planes, repairs, repairs // racks)
        buffers = [
            pltpu.VMEM((hold * planes, width), jnp.float32)
            for _ in range(2)
            for _, width, _ in groups
        ]
        for order, _, width in tasks:
            for stage in range(len(counts) + 1):
                left = [counts[a] for a in counts if a not in order[:stage]]
                if stage:
                    left = [counts[order[stage - 1]] - 1] + left
                buffers.append(pltpu.VMEM((*left, out_rows, width), jnp.float32))
        most = max(counts.values()) - 1
        dma = pltpu.SemaphoreType.DMA
        hbm = pl.BlockSpec(memory_space=pltpu.HBM)
        operands = (
            helper_rack.T,
            helper_node.T,
            helper_block.T,
            coefficients.transpose(1, 2, 3, 0),
            stored.reshape(hold * planes, length),
        )
        buffer_bytes = sum(math.prod(b.shape) * 4 for b in buffers)
        rebuilt = pl.pallas_call(
            functools.partial(repair_kernel, sizes, groups),
            out_shape=jax.ShapeDtypeStruct((out_rows, length), jnp.float32),
            in_specs=[hbm] * 5,
            out_specs=pl.BlockSpec(memory_space=pltpu.VMEM),
            scratch_shapes=[
                *[pltpu.VMEM(a.shape, a.dtype) for a in operands],
                dma((len(operands),)),
                pltpu.VMEM((2, repairs * planes // CORES, hold * planes), jnp.bfloat16),
                dma((len(groups),)),
                dma((len(groups),)),
                dma((len(tasks), len(counts), most)),
                dma((len(tasks), len(counts), most)),
                *buffers,
            ],
            compiler_params=pltpu.CompilerParams(
                collective_id=0,
                has_side_effects=True,
                vmem_limit_bytes=max(buffer_bytes + 12 * 2**20, 56 * 2**20),
            ),
        )(*operands)
        return rebuilt.reshape(-1, planes, length)

    return jax.shard_map(
        on_device,
        mesh=mesh,
        in_specs=(P(("rack", "node"), None, None), P(), P(), P(), P()),
        out_specs=P(("rack", "node"), None, None),
        check_vma=False,
    )
```
